256 devices in a mesh: band: 32 (over x, y, core), grp: 8 (over z).
Axes of the slice: x: 4, y: 4, z: 8, core: 2. Of those that a mesh axis runs over, the one named last changes fastest.
Arguments:
- composition: float32 [1048576, 160], P(('band', 'grp')), may hold values from -3 to 3
- neighbours: int32 [8192, 3], P(('band', 'grp')), may hold values from 0 to 255
- mixing_weights: bfloat16 [8192, 3, 128, 128], P(('band', 'grp')), may hold values from -0.3125 to 0.3125
- slot_order: int32 [256, 4096], P(('band', 'grp')), may hold values from 0 to 4095, each once within a row
- photo_index: int32 [1048576], P(('band', 'grp')), may hold values from 0 to 63
- photo_table: float32 [64, 160], replicated, may hold values from 0.05 to 1
- coupling: float32 [160, 160], replicated, may hold values from -0.5 to 0.5
- loss_rate: float32 [160], replicated, may hold values from 0.05 to 0.5
- preconditioner: float32 [8192, 160, 160], P(('band', 'grp')), may hold values from -0.25 to 1.25
Outputs:
- updated: float32 [1048576, 160], P(('band', 'grp'))
The draws below stay inside these ranges and needn't reach their ends.
All inputs are finite; a program needn't handle non-finite values.
Results may differ from the reference program's by a relative error of at most 0.0022.
Values may be sent and summed in bfloat16 or wider, within the bound.
No kernel may reach another device: no remote copies, remote signals or barrier semaphores. Data moves between devices by JAX's collectives and lax.ppermute only.
A program may use at most 128 MiB of HBM per device.

```python
import math
import jax
import jax.numpy as jnp
from jax import lax

SPECIES = 160
BLOCK = 128
NEIGH = 3
NEWTON = 2
LEVELS = 64
BLK_DEV = 32
P_DEV = 4096
BLOCKS = 8192
PARCELS = 1048576
SHARE = 128
N_BAND = 32
N_GRP = 8


def draw_preconditioner(key, part):
    key = jax.random.fold_in(key, 7)
    shape = (BLK_DEV * N_BAND * N_GRP, SPECIES, SPECIES)
    noise = jnp.clip(jax.random.normal(key, shape, jnp.float32), -3.0, 3.0)
    return jnp.eye(SPECIES, dtype=jnp.float32) + noise * (0.4 / SPECIES ** 0.5)


def touch_ends(result, own_key, low, largest):
    shape = result.shape
    spot = [jax.random.randint(jax.random.fold_in(own_key, axis), (), 0, shape[axis]) for axis in range(len(shape))]
    result = result.at[tuple(spot)].set(low)
    longest = shape.index(max(shape))
    spot[longest] = (spot[longest] + 1) % shape[longest]
    return result.at[tuple(spot)].set(largest)


def block_scale(rng, extent, split, smallest, top_value):
    def one(axis_at, blocks):
        draws = jax.random.uniform(jax.random.fold_in(jax.random.fold_in(rng, 6), axis_at), (blocks,), jnp.float32, smallest / len(split), top_value / len(split))
        return jnp.repeat(jnp.exp(draws), extent[axis_at] // blocks).reshape((-1,) + (1,) * (len(extent) - axis_at - 1))

    gain = one(*split[0])
    for cut in split[1:]:
        gain = gain * one(*cut)
    return gain


def normal_values(stream_key, dims, scale, reach, pieces=(), kind=jnp.bfloat16):
    result = jax.random.normal(stream_key, dims, jnp.float32) * scale
    if len(pieces) > 0:
        result = block_scale(stream_key, dims, pieces, -0.22, 0.18) * result
    return jnp.clip(result, min=-reach, max=reach).astype(kind)


def setup_inputs(seed: int = 0) -> dict:
    arg_keys = jax.random.split(jax.random.key(seed), 10)
    composition = normal_values(arg_keys[0], (PARCELS, SPECIES), 0.5, 3.0, ((0, 256),), jnp.float32)
    neighbours = touch_ends(jax.random.randint(arg_keys[1], (BLOCKS, NEIGH), 0, BLK_DEV * N_GRP), jax.random.fold_in(arg_keys[1], 1), 0, (BLK_DEV * N_GRP) - 1).astype(jnp.int32)
    mixing_weights = normal_values(arg_keys[2], (BLOCKS, NEIGH, BLOCK, BLOCK), (NEIGH * BLOCK) ** -0.5, 0.3125, ((0, 256),))
    slot_order = jax.vmap(lambda own: jax.random.permutation(own, P_DEV))(jax.random.split(arg_keys[3], (N_BAND * N_GRP))).reshape((N_BAND * N_GRP, P_DEV)).astype(jnp.int32)
    photo_index = touch_ends(jax.random.randint(arg_keys[4], (PARCELS,), 0, LEVELS), jax.random.fold_in(arg_keys[4], 1), 0, LEVELS - 1).astype(jnp.int32)
    photo_table = jnp.clip(jnp.exp(jax.random.uniform(arg_keys[5], (LEVELS, SPECIES), jnp.float32, math.log(0.05), math.log(1.0))), 0.05, 1.0)
    coupling = normal_values(arg_keys[6], (SPECIES, SPECIES), SPECIES ** -0.5, 0.5, (), jnp.float32)
    loss_rate = jnp.clip(jnp.exp(jax.random.uniform(arg_keys[7], (SPECIES,), jnp.float32, math.log(0.05), math.log(0.5))), 0.05, 0.5)
    preconditioner = draw_preconditioner(jax.random.fold_in(arg_keys[9], 71), 0)
    return dict(composition=composition, neighbours=neighbours, mixing_weights=mixing_weights, slot_order=slot_order, photo_index=photo_index, photo_table=photo_table, coupling=coupling, loss_rate=loss_rate, preconditioner=preconditioner)


time_step = 0.5


def band_mix(inputs):
    own_blocks, rounded_blocks, lists, weights = inputs
    picked = jnp.take(rounded_blocks, lists, axis=0).astype(jnp.float32)
    mixing_term = jnp.einsum("bkpq,bkqs->bps", weights.astype(jnp.float32), picked)
    return own_blocks + mixing_term


def place_slots(values, slots):
    return jnp.zeros_like(values).at[slots].set(values)


def read_slots(values, slots):
    return jnp.take(values, slots, axis=0)


def reference(composition, neighbours, mixing_weights, slot_order, photo_index, photo_table, coupling, loss_rate, preconditioner):
    band_blocks = N_GRP * BLK_DEV
    blocks_all = composition.reshape(N_BAND, band_blocks, BLOCK, SPECIES)
    rounded = blocks_all.astype(jnp.bfloat16)
    lists = neighbours.reshape(N_BAND, band_blocks, NEIGH).astype(jnp.int32)
    weights = mixing_weights.reshape(N_BAND, band_blocks, NEIGH, BLOCK, BLOCK)
    mixed = lax.map(band_mix, (blocks_all, rounded, lists, weights))
    mixed = mixed.reshape(N_BAND, N_GRP, P_DEV, SPECIES)
    slots = slot_order.reshape(N_BAND, N_GRP, P_DEV).astype(jnp.int32)
    outgoing = jax.vmap(jax.vmap(place_slots))(mixed, slots)
    start = outgoing.reshape(N_BAND, N_GRP, N_BAND, SHARE, SPECIES).transpose(2, 1, 0, 3, 4).reshape(PARCELS, SPECIES)
    photo_rates = jnp.take(photo_table, photo_index.astype(jnp.int32), axis=0)
    current = start
    for newton_step in range(NEWTON):
        forcing = jnp.dot(current * photo_rates, coupling, precision=lax.Precision.HIGHEST) - loss_rate * current * current
        defect = current - start - time_step * forcing
        update = jnp.einsum("tps,tsq->tpq", defect.reshape(BLOCKS, BLOCK, SPECIES), preconditioner, precision=lax.Precision.HIGHEST)
        current = current - update.reshape(PARCELS, SPECIES)
    returned = current.reshape(N_BAND, N_GRP, N_BAND, SHARE, SPECIES).transpose(2, 1, 0, 3, 4).reshape(N_BAND, N_GRP, P_DEV, SPECIES)
    updated = jax.vmap(jax.vmap(read_slots))(returned, slots)
    return updated.reshape(PARCELS, SPECIES)
```

```python
import functools

import jax
import jax.numpy as jnp
from jax import lax
from jax.experimental import pallas as pl
from jax.experimental.pallas import tpu as pltpu
from jax.sharding import PartitionSpec as P

BLOCK = 128
NEWTON = 2
WIDE = 256
time_step = 0.5

f32 = jnp.float32
bf16 = jnp.bfloat16
VMEM = pl.BlockSpec(memory_space=pltpu.VMEM)
SMEM = pl.BlockSpec(memory_space=pltpu.SMEM)
ANY = pl.BlockSpec(memory_space=pl.ANY)


def params(mib):
    return pltpu.CompilerParams(vmem_limit_bytes=mib << 20)


def halves(values):
    high = values.astype(bf16)
    return high, (values - high.astype(f32)).astype(bf16)


def pack_kernel(tiles_ref, photo_ref, out_ref):
    count, species, _ = tiles_ref.shape

    def body(t, _):
        out_ref[t, pl.ds(0, species), :] = tiles_ref[t].T
        entries = photo_ref[pl.ds(t, 1), :].astype(f32)
        row = jnp.concatenate([entries, jnp.zeros((1, species - BLOCK), f32)], axis=1)
        out_ref[t, pl.ds(species, 8), :] = jnp.broadcast_to(row, (8, species))
        return 0

    lax.fori_loop(0, count, body, 0)


def pack(tiles, photo):
    count, species, _ = tiles.shape
    return pl.pallas_call(
        pack_kernel,
        out_shape=jax.ShapeDtypeStruct((count, species + 8, species), f32),
        in_specs=[VMEM, VMEM],
        out_specs=VMEM,
        compiler_params=params(32),
    )(tiles, photo)


def unpack_kernel(packed_ref, table_ref, high_ref, low_ref, rates_ref):
    count, _, species = packed_ref.shape
    levels = table_ref.shape[1]
    t_high, t_rest = halves(table_ref[...])
    first = table_ref[...] - t_high.astype(f32)
    t_low = (first - t_rest.astype(f32)).astype(bf16)

    def body(t, _):
        high, low = halves(packed_ref[t, pl.ds(0, species), :])
        high_ref[t] = high
        low_ref[t] = low
        entries = packed_ref[t, pl.ds(species, 1), pl.ds(0, BLOCK)].astype(jnp.int32)
        level = lax.broadcasted_iota(jnp.int32, (levels, BLOCK), 0)
        onehot = (level == entries).astype(f32).astype(bf16)
        rates = jnp.dot(t_high, onehot, preferred_element_type=f32)
        rates += jnp.dot(t_rest, onehot, preferred_element_type=f32)
        rates += jnp.dot(t_low, onehot, preferred_element_type=f32)
        rates_ref[:, pl.ds(pl.multiple_of(t * BLOCK, BLOCK), BLOCK)] = rates
        return 0

    lax.fori_loop(0, count, body, 0)


def unpack(packed, table):
    count, _, species = packed.shape
    return pl.pallas_call(
        unpack_kernel,
        out_shape=(
            jax.ShapeDtypeStruct((count, species, species), bf16),
            jax.ShapeDtypeStruct((count, species, species), bf16),
            jax.ShapeDtypeStruct((species, count * BLOCK), f32),
        ),
        in_specs=[VMEM, VMEM],
        out_specs=(VMEM, VMEM, VMEM),
        compiler_params=params(32),
    )(packed, table)


def select_kernel(slots_ref, out_ref):
    parcels = slots_ref.shape[1]

    def body(t, _):
        off = pl.multiple_of(t * WIDE, WIDE)
        place = slots_ref[:, pl.ds(off, WIDE)] & (WIDE - 1)
        lane = lax.broadcasted_iota(jnp.int32, (WIDE, WIDE), 0)
        out_ref[pl.ds(off, WIDE), :] = (lane == place).astype(f32).T.astype(bf16)
        return 0

    lax.fori_loop(0, parcels // WIDE, body, 0)


def select(slots):
    parcels = slots.shape[1]
    return pl.pallas_call(
        select_kernel,
        out_shape=jax.ShapeDtypeStruct((parcels, WIDE), bf16),
        in_specs=[VMEM],
        out_specs=VMEM,
        compiler_params=params(16),
    )(slots)


def mix_kernel(first, size, *refs):
    codes_ref, weights_ref, comp_ref, slots_ref, select_ref = refs[:5]
    parts = refs[5:14]
    mixed_ref, start_ref, held, own, stack, sems = refs[14:]
    parcels = mixed_ref.shape[1]
    blocks = parcels // BLOCK
    wide = parcels // WIDE
    half = size // 2
    copies = [
        pltpu.make_async_copy(comp_ref.at[pl.ds(first, size), :], own, sems.at[9])
    ]
    for place in range(7):
        spot = place if place < 4 else place + 1
        copies.append(pltpu.make_async_copy(parts[place], held.at[spot], sems.at[place]))
    copies.append(
        pltpu.make_async_copy(parts[7], held.at[4, pl.ds(0, half), :], sems.at[7])
    )
    copies.append(
        pltpu.make_async_copy(parts[8], held.at[4, pl.ds(half, half), :], sems.at[8])
    )
    for copy in copies:
        copy.start()
    for copy in copies:
        copy.wait()

    def mix(c, _):
        picked = []
        for k in range(weights_ref.shape[1]):
            code = codes_ref[c, k]
            column = pl.multiple_of((code & (blocks - 1)) * BLOCK, BLOCK)
            picked.append(held[lax.div(code, blocks), :, pl.ds(column, BLOCK)])
        rows = jnp.concatenate(picked, axis=1)
        weights = jnp.concatenate(
            [weights_ref[c, k] for k in range(weights_ref.shape[1])], axis=1
        )
        term = lax.dot_general(
            rows, weights, (((1,), (1,)), ((), ())), preferred_element_type=f32
        )
        off = pl.multiple_of(c * BLOCK, BLOCK)
        mixed_ref[:, pl.ds(off, BLOCK)] = own[:, pl.ds(off, BLOCK)] + term
        return 0

    lax.fori_loop(0, blocks, mix, 0, unroll=4)
    high, low = halves(mixed_ref[...])
    both = jnp.concatenate([high, low], axis=0)
    group = slots_ref[...] >> 8
    for j in range(wide):
        keep = (group == j).astype(f32).astype(bf16)
        stack[pl.ds(j * 2 * size, 2 * size), :] = both * keep
    moved = jnp.dot(stack[...], select_ref[...], preferred_element_type=f32)
    for j in range(wide):
        at = j * 2 * size
        start_ref[:, pl.ds(j * WIDE, WIDE)] = moved[at : at + size] + moved[at + size : at + 2 * size]


def mix(first, size, codes, weights, comp, slots, chosen, parts):
    parcels = comp.shape[1]
    shape = jax.ShapeDtypeStruct((size, parcels), f32)
    return pl.pallas_call(
        functools.partial(mix_kernel, first, size),
        out_shape=(shape, shape),
        in_specs=[SMEM, VMEM, ANY, VMEM, VMEM] + [ANY] * 9,
        out_specs=(VMEM, VMEM),
        scratch_shapes=[
            pltpu.VMEM((8, size, parcels), bf16),
            pltpu.VMEM((size, parcels), f32),
            pltpu.VMEM((parcels // WIDE * 2 * size, parcels), bf16),
            pltpu.SemaphoreType.DMA((10,)),
        ],
        compiler_params=params(40),
    )(codes, weights, comp, slots, chosen, *parts)


def chem_kernel(sizes, *refs):
    count = len(sizes)
    starts, mixes = refs[:count], refs[count : 2 * count]
    rates_ref, high_ref, low_ref, yields_ref, loss_ref, slots_ref = refs[2 * count : 2 * count + 6]
    out_ref, begun, delta = refs[2 * count + 6 :]
    species, parcels = rates_ref.shape
    tiles = parcels // BLOCK
    wide = parcels // WIDE
    at = 0
    for ref, size in zip(starts, sizes):
        begun[pl.ds(at, size), :] = ref[...]
        at += size
    y_high, y_low = halves(yields_ref[...])
    loss = loss_ref[...]

    def product(m_high, m_low, values):
        high, low = halves(values)
        total = jnp.dot(m_high, high, preferred_element_type=f32)
        total += jnp.dot(m_high, low, preferred_element_type=f32)
        return total + jnp.dot(m_low, high, preferred_element_type=f32)

    def chem(t, _):
        off = pl.multiple_of(t * BLOCK, BLOCK)
        start = begun[:, pl.ds(off, BLOCK)]
        rates = rates_ref[:, pl.ds(off, BLOCK)]
        m_high, m_low = high_ref[t], low_ref[t]
        current = start
        for newton_step in range(NEWTON):
            forcing = product(y_high, y_low, current * rates) - loss * current * current
            defect = current - start - time_step * forcing
            current = current - product(m_high, m_low, defect)
        delta[lax.div(t, 2), :, pl.ds(pl.multiple_of((t & 1) * BLOCK, BLOCK), BLOCK)] = (
            current - start
        ).astype(bf16)
        return 0

    lax.fori_loop(0, tiles, chem, 0, unroll=2)

    def back(t, _):
        off = pl.multiple_of(t * WIDE, WIDE)
        slots = slots_ref[:, pl.ds(off, WIDE)]
        lane = lax.broadcasted_iota(jnp.int32, (WIDE, WIDE), 0)
        chosen = (lane == (slots & (WIDE - 1))).astype(f32).astype(bf16)
        group = slots >> 8
        total = jnp.zeros((species, WIDE), f32)
        for j in range(wide):
            moved = jnp.dot(delta[j], chosen, preferred_element_type=f32)
            total = jnp.where(group == j, moved, total)
        at = 0
        for ref, size in zip(mixes, sizes):
            out_ref[pl.ds(at, size), pl.ds(off, WIDE)] = (
                ref[:, pl.ds(off, WIDE)] + total[at : at + size]
            )
            at += size
        return 0

    lax.fori_loop(0, wide, back, 0)


def chem(sizes, starts, mixes, rates, high, low, yields, loss, slots):
    species, parcels = rates.shape
    return pl.pallas_call(
        functools.partial(chem_kernel, sizes),
        out_shape=jax.ShapeDtypeStruct((species, parcels), f32),
        in_specs=[VMEM] * (2 * len(sizes) + 6),
        out_specs=VMEM,
        scratch_shapes=[
            pltpu.VMEM((species, parcels), f32),
            pltpu.VMEM((parcels // WIDE, species, WIDE), bf16),
        ],
        compiler_params=params(48),
    )(*starts, *mixes, rates, high, low, yields, loss, slots)


def ring(own, size):
    right = [(i, (i + 1) % size) for i in range(size)]
    left = [(i, (i - 1) % size) for i in range(size)]
    half = own.shape[0] // 2
    from_left = from_right = own
    lefts, rights = [], []
    for _ in range(size // 2 - 1):
        from_left = lax.ppermute(from_left, "grp", right)
        from_right = lax.ppermute(from_right, "grp", left)
        lefts.append(from_left)
        rights.append(from_right)
    far_top = lax.ppermute(from_left[:half], "grp", right)
    far_bottom = lax.ppermute(from_right[half:], "grp", left)
    return [own] + lefts + rights[::-1] + [far_top, far_bottom]


SIZES = (32, 32, 32, 32, 32)


def shards(
    composition,
    neighbours,
    mixing_weights,
    slot_order,
    photo_index,
    photo_table,
    coupling,
    loss_rate,
    preconditioner,
):
    parcels, species = composition.shape
    blocks = parcels // BLOCK
    ring_size = lax.axis_size("grp")
    comp = composition.T
    firsts = [sum(SIZES[:i]) for i in range(len(SIZES))]
    rings = []
    for first, size in zip(firsts, SIZES):
        rings.append(ring(comp[first : first + size].astype(bf16), ring_size))
    packed = pack(preconditioner, photo_index.reshape(blocks, BLOCK))
    arrived = lax.all_to_all(packed, "band", split_axis=0, concat_axis=0, tiled=True)
    chosen = select(slot_order)
    high, low, rates = unpack(arrived, photo_table.T)
    distance = (lax.axis_index("grp") - neighbours // blocks) % ring_size
    codes = distance * blocks + neighbours % blocks
    mixes, starts = [], []
    for first, size, parts in zip(firsts, SIZES, rings):
        mixed, start = mix(first, size, codes, mixing_weights, comp, slot_order, chosen, parts)
        mixes.append(mixed)
        starts.append(start)
    updated = chem(
        SIZES, starts, mixes, rates, high, low, coupling.T, loss_rate.reshape(species, 1), slot_order
    )
    return updated.T


def solution(mesh):
    placed = (
        P(("band", "grp"), None),
        P(("band", "grp"), None),
        P(("band", "grp"), None, None, None),
        P(("band", "grp"), None),
        P(("band", "grp")),
        P(),
        P(),
        P(),
        P(("band", "grp"), None, None),
    )
    return jax.shard_map(
        shards, mesh=mesh, in_specs=placed, out_specs=P(("band", "grp"), None), check_vma=False
    )
```

```python
import functools

import jax
import jax.numpy as jnp
from jax import lax
from jax.experimental import pallas as pl
from jax.experimental.pallas import tpu as pltpu
from jax.sharding import PartitionSpec as P

BLOCK = 128
NEWTON = 2
WIDE = 256
LIMIT = 60
GROUPS = 4
LOT = 8
time_step = 0.5

f32 = jnp.float32
bf16 = jnp.bfloat16
VMEM = pl.BlockSpec(memory_space=pltpu.VMEM)
SMEM = pl.BlockSpec(memory_space=pltpu.SMEM)
ANY = pl.BlockSpec(memory_space=pl.ANY)


CHEAP = pl.CostEstimate(flops=1, bytes_accessed=1, transcendentals=0)


def params(mib):
    return pltpu.CompilerParams(vmem_limit_bytes=mib << 20)


def halves(values):
    high = values.astype(bf16)
    return high, (values - high.astype(f32)).astype(bf16)


def pack_kernel(tiles_ref, photo_ref, out_ref):
    count, species, _ = tiles_ref.shape
    rest = species - BLOCK
    fold = BLOCK // rest
    rows = species // fold

    def body(t, _):
        tile = tiles_ref[t].T
        out_ref[t, pl.ds(0, species), :] = tile[:, :BLOCK]
        out_ref[t, pl.ds(species, rows), :] = jnp.concatenate(
            [tile[i * rows : (i + 1) * rows, BLOCK:] for i in range(fold)], axis=1
        )
        entries = photo_ref[pl.ds(t, 1), :].astype(f32)
        out_ref[t, pl.ds(species + rows, 8), :] = jnp.broadcast_to(entries, (8, BLOCK))
        return 0

    lax.fori_loop(0, count, body, 0, unroll=2)


def pack(tiles, photo):
    count, species, _ = tiles.shape
    rows = species + species * (species - BLOCK) // BLOCK + 8
    return pl.pallas_call(
        pack_kernel,
        out_shape=jax.ShapeDtypeStruct((count, rows, BLOCK), f32),
        grid=(count // LOT,),
        in_specs=[
            pl.BlockSpec((LOT, species, species), lambda i: (i, 0, 0)),
            pl.BlockSpec((LOT, BLOCK), lambda i: (i, 0)),
        ],
        out_specs=pl.BlockSpec((LOT, rows, BLOCK), lambda i: (i, 0, 0)),
        compiler_params=params(LIMIT),
        cost_estimate=CHEAP,
    )(tiles, photo)


def unpack_kernel(packed_ref, table_ref, tiles_ref, rates_ref):
    count = packed_ref.shape[0]
    species = rates_ref.shape[0]
    levels = table_ref.shape[1]
    rest = species - BLOCK
    fold = BLOCK // rest
    rows = species // fold
    t_high, t_rest = halves(table_ref[...])
    first = table_ref[...] - t_high.astype(f32)
    t_low = (first - t_rest.astype(f32)).astype(bf16)
    table = jnp.concatenate([t_high, t_rest, t_low], axis=1)

    def body(t, _):
        folded = packed_ref[t, pl.ds(species, rows), :]
        tail = jnp.concatenate(
            [folded[:, i * rest : (i + 1) * rest] for i in range(fold)], axis=0
        )
        tile = jnp.concatenate([packed_ref[t, pl.ds(0, species), :], tail], axis=1)
        high, low = halves(tile)
        tiles_ref[t] = jnp.concatenate([high, low, high], axis=1)
        entries = packed_ref[t, pl.ds(species + rows, 1), :].astype(jnp.int32)
        level = lax.broadcasted_iota(jnp.int32, (levels, BLOCK), 0)
        onehot = (level == entries).astype(f32).astype(bf16)
        onehot = jnp.concatenate([onehot, onehot, onehot], axis=0)
        rates_ref[:, pl.ds(pl.multiple_of(t * BLOCK, BLOCK), BLOCK)] = jnp.dot(
            table, onehot, preferred_element_type=f32
        )
        return 0

    lax.fori_loop(0, count, body, 0, unroll=2)


def unpack(packed, table):
    count = packed.shape[0]
    species = table.shape[0]
    return pl.pallas_call(
        unpack_kernel,
        out_shape=(
            jax.ShapeDtypeStruct((count, species, 3 * species), bf16),
            jax.ShapeDtypeStruct((species, count * BLOCK), f32),
        ),
        grid=(count // LOT,),
        in_specs=[
            pl.BlockSpec((LOT,) + packed.shape[1:], lambda i: (i, 0, 0)),
            pl.BlockSpec(table.shape, lambda i: (0, 0)),
        ],
        out_specs=(
            pl.BlockSpec((LOT, species, 3 * species), lambda i: (i, 0, 0)),
            pl.BlockSpec((species, LOT * BLOCK), lambda i: (0, i)),
        ),
        compiler_params=params(LIMIT),
        cost_estimate=CHEAP,
    )(packed, table)


def select_kernel(slots_ref, out_ref):
    parcels = slots_ref.shape[1]

    def body(t, _):
        off = pl.multiple_of(t * WIDE, WIDE)
        place = slots_ref[:, pl.ds(off, WIDE)] & (WIDE - 1)
        lane = lax.broadcasted_iota(jnp.int32, (WIDE, WIDE), 0)
        out_ref[pl.ds(off, WIDE), :] = (lane == place).astype(f32).T.astype(bf16)
        return 0

    lax.fori_loop(0, parcels // WIDE, body, 0)


def select(slots):
    parcels = slots.shape[1]
    return pl.pallas_call(
        select_kernel,
        out_shape=jax.ShapeDtypeStruct((parcels, WIDE), bf16),
        in_specs=[VMEM],
        out_specs=VMEM,
        compiler_params=params(LIMIT),
        cost_estimate=CHEAP,
    )(slots)


def mix_kernel(first, size, count, *refs):
    codes_ref, slots_ref, weights_ref, comp_ref, select_ref = refs[:5]
    parts = refs[5 : 5 + count]
    mixed_ref, start_ref, held, own, weights, chosen, both, stack, sems = refs[5 + count :]
    parcels = mixed_ref.shape[1]
    blocks = parcels // BLOCK
    wide = parcels // WIDE
    half = size // 32 * 16
    lots = 4
    lot = blocks // lots
    copies = []
    for place in range(7):
        spot = place if place < 4 else place + 1
        copies.append((parts[place], held.at[spot]))
    copies.append((parts[7], held.at[4, pl.ds(0, half), :]))
    copies.append((parts[8], held.at[4, pl.ds(half, size - half), :]))
    copies.append((comp_ref.at[pl.ds(first, size), :], own))
    early = len(copies)
    for n in range(lots):
        copies.append((weights_ref.at[pl.ds(n * lot, lot)], weights.at[pl.ds(n * lot, lot)]))
    copies.append((select_ref, chosen))
    copies = [
        pltpu.make_async_copy(source, target, sems.at[i])
        for i, (source, target) in enumerate(copies)
    ]
    for copy in copies:
        copy.start()
    for copy in copies[:early]:
        copy.wait()

    def mix(c, _):
        picked = []
        for k in range(weights.shape[1]):
            code = codes_ref[c, k]
            column = pl.multiple_of((code & (blocks - 1)) * BLOCK, BLOCK)
            picked.append(held[lax.div(code, blocks), :, pl.ds(column, BLOCK)])
        rows = jnp.concatenate(picked, axis=1)
        block = jnp.concatenate([weights[c, k] for k in range(weights.shape[1])], axis=1)
        term = lax.dot_general(
            rows, block, (((1,), (1,)), ((), ())), preferred_element_type=f32
        )
        off = pl.multiple_of(c * BLOCK, BLOCK)
        mixed_ref[:, pl.ds(off, BLOCK)] = own[:, pl.ds(off, BLOCK)] + term
        return 0

    for n in range(lots):
        copies[early + n].wait()
        lax.fori_loop(n * lot, (n + 1) * lot, mix, 0, unroll=lot)
    high, low = halves(mixed_ref[...])
    both[pl.ds(0, size), :] = high
    both[pl.ds(size, size), :] = low
    copies[early + lots].wait()

    def move(i, _):
        group = slots_ref[...] >> 8
        for j in range(GROUPS):
            keep = (group == i * GROUPS + j).astype(f32).astype(bf16)
            stack[pl.ds(j * 2 * size, 2 * size), :] = both[...] * keep
        moved = jnp.dot(stack[...], chosen[...], preferred_element_type=f32)
        for j in range(GROUPS):
            at = j * 2 * size
            off = pl.multiple_of((i * GROUPS + j) * WIDE, WIDE)
            start_ref[:, pl.ds(off, WIDE)] = (
                moved[at : at + size] + moved[at + size : at + 2 * size]
            )
        return 0

    lax.fori_loop(0, wide // GROUPS, move, 0)


def mix(first, size, codes, weights, comp, slots, chosen, parts):
    parcels = comp.shape[1]
    shape = jax.ShapeDtypeStruct((size, parcels), f32)
    return pl.pallas_call(
        functools.partial(mix_kernel, first, size, len(parts)),
        out_shape=(shape, shape),
        in_specs=[SMEM, VMEM] + [ANY] * (3 + len(parts)),
        out_specs=(VMEM, VMEM),
        scratch_shapes=[
            pltpu.VMEM((8, size, parcels), bf16),
            pltpu.VMEM((size, parcels), f32),
            pltpu.VMEM(weights.shape, bf16),
            pltpu.VMEM(chosen.shape, bf16),
            pltpu.VMEM((2 * size, parcels), bf16),
            pltpu.VMEM((GROUPS * 2 * size, parcels), bf16),
            pltpu.SemaphoreType.DMA((15,)),
        ],
        compiler_params=params(LIMIT),
        cost_estimate=CHEAP,
    )(codes, slots, weights, comp, chosen, *parts)


BATCH = 4


def finish_kernel(
    near_ref, slots_ref, yields_ref, loss_ref,
    gathered_ref, weights_ref, comp_ref, select_ref, mixed_ref, start_ref, rates_ref, tiles_ref,
    out_ref,
    held, weights, chosen, home, both, stack, begun, rates_in, tiles, delta, result,
    sems, lot_sems, out_sems,
):
    species, parcels = rates_in.shape
    size = held.shape[1]
    blocks = parcels // BLOCK
    wide = parcels // WIDE
    span = BATCH * BLOCK
    batches = parcels // span
    lots = 4
    lot = blocks // lots
    rest = species - size
    first_copies = [
        pltpu.make_async_copy(gathered_ref, held, sems.at[0]),
        pltpu.make_async_copy(
            comp_ref.at[pl.ds(0, size), :], home.at[pl.ds(0, size), :], sems.at[1]
        ),
    ]
    weight_copies = [
        pltpu.make_async_copy(
            weights_ref.at[pl.ds(n * lot, lot)], weights.at[pl.ds(n * lot, lot)], sems.at[2 + n]
        )
        for n in range(lots)
    ]
    select_copy = pltpu.make_async_copy(select_ref, chosen, sems.at[2 + lots])
    home_copy = pltpu.make_async_copy(
        mixed_ref, home.at[pl.ds(size, rest), :], sems.at[3 + lots]
    )
    start_copy = pltpu.make_async_copy(
        start_ref, begun.at[pl.ds(size, rest), :], sems.at[4 + lots]
    )
    lot_copies = []
    for b in range(batches):
        column = pl.ds(b * span, span)
        lot_copies.append(
            pltpu.make_async_copy(
                rates_ref.at[:, column], rates_in.at[:, column], lot_sems.at[b, 0]
            )
        )
        lot_copies.append(
            pltpu.make_async_copy(
                tiles_ref.at[pl.ds(b * BATCH, BATCH)],
                tiles.at[pl.ds(b * BATCH, BATCH)],
                lot_sems.at[b, 1],
            )
        )
    for copy in (
        first_copies + weight_copies + [select_copy, start_copy] + lot_copies + [home_copy]
    ):
        copy.start()
    for copy in first_copies:
        copy.wait()

    def mix(c, _):
        picked = []
        for k in range(weights.shape[1]):
            block = near_ref[c, k]
            column = pl.multiple_of((block & (blocks - 1)) * BLOCK, BLOCK)
            picked.append(held[lax.div(block, blocks), :, pl.ds(column, BLOCK)])
        rows = jnp.concatenate(picked, axis=1)
        block = jnp.concatenate([weights[c, k] for k in range(weights.shape[1])], axis=1)
        term = lax.dot_general(
            rows, block, (((1,), (1,)), ((), ())), preferred_element_type=f32
        )
        off = pl.multiple_of(c * BLOCK, BLOCK)
        total = home[pl.ds(0, size), pl.ds(off, BLOCK)] + term
        home[pl.ds(0, size), pl.ds(off, BLOCK)] = total
        high, low = halves(total)
        both[pl.ds(0, size), pl.ds(off, BLOCK)] = high
        both[pl.ds(size, size), pl.ds(off, BLOCK)] = low
        return 0

    for n in range(lots):
        weight_copies[n].wait()
        lax.fori_loop(n * lot, (n + 1) * lot, mix, 0, unroll=lot)
    select_copy.wait()

    def move(i, _):
        group = slots_ref[...] >> 8
        for j in range(GROUPS):
            keep = (group == i * GROUPS + j).astype(f32).astype(bf16)
            stack[pl.ds(j * 2 * size, 2 * size), :] = both[...] * keep
        moved = jnp.dot(stack[...], chosen[...], preferred_element_type=f32)
        for j in range(GROUPS):
            at = j * 2 * size
            off = pl.multiple_of((i * GROUPS + j) * WIDE, WIDE)
            begun[pl.ds(0, size), pl.ds(off, WIDE)] = (
                moved[at : at + size] + moved[at + size : at + 2 * size]
            )
        return 0

    lax.fori_loop(0, wide // GROUPS, move, 0)
    start_copy.wait()
    y_high, y_low = halves(yields_ref[...])
    yields = jnp.concatenate([y_high, y_low, y_high], axis=1)
    loss = loss_ref[...]

    def spread(values):
        high, low = halves(values)
        return jnp.concatenate([high, high, low], axis=0)

    for b in range(batches):
        lot_copies[2 * b].wait()
        lot_copies[2 * b + 1].wait()
        off = b * span
        start = begun[:, pl.ds(off, span)]
        rates = rates_in[:, pl.ds(off, span)]
        current = start
        for newton_step in range(NEWTON):
            forcing = (
                jnp.dot(yields, spread(current * rates), preferred_element_type=f32)
                - loss * current * current
            )
            defect = current - start - time_step * forcing
            wings = spread(defect)
            update = [
                jnp.dot(
                    tiles[b * BATCH + i],
                    wings[:, i * BLOCK : (i + 1) * BLOCK],
                    preferred_element_type=f32,
                )
                for i in range(BATCH)
            ]
            current = current - jnp.concatenate(update, axis=1)
        change = (current - start).astype(bf16)
        for i in range(span // WIDE):
            delta[pl.ds((b * span // WIDE + i) * species, species), :] = change[
                :, i * WIDE : (i + 1) * WIDE
            ]

    home_copy.wait()
    outs = []
    for t in range(wide):
        off = t * WIDE
        slots = slots_ref[:, pl.ds(off, WIDE)]
        lane = lax.broadcasted_iota(jnp.int32, (WIDE, WIDE), 0)
        picks = (lane == (slots & (WIDE - 1))).astype(f32).astype(bf16)
        group = slots >> 8
        total = jnp.zeros((species, WIDE), f32)
        for j in range(wide):
            moved = jnp.dot(
                delta[pl.ds(j * species, species), :], picks, preferred_element_type=f32
            )
            total = jnp.where(group == j, moved, total)
        result[:, pl.ds(off, WIDE)] = home[:, pl.ds(off, WIDE)] + total
        out = pltpu.make_async_copy(
            result.at[:, pl.ds(off, WIDE)], out_ref.at[:, pl.ds(off, WIDE)], out_sems.at[t]
        )
        out.start()
        outs.append(out)
    for out in outs:
        out.wait()


def finish(neighbours, slots, yields, loss, gathered, weights, comp, chosen, mixed, start, rates, tiles):
    species, parcels = rates.shape
    size = gathered.shape[1]
    batches = parcels // (BATCH * BLOCK)
    whole = pltpu.VMEM((species, parcels), f32)
    return pl.pallas_call(
        finish_kernel,
        out_shape=jax.ShapeDtypeStruct((species, parcels), f32),
        in_specs=[SMEM] + [VMEM] * 3 + [ANY] * 8,
        out_specs=ANY,
        scratch_shapes=[
            pltpu.VMEM(gathered.shape, bf16),
            pltpu.VMEM(weights.shape, bf16),
            pltpu.VMEM(chosen.shape, bf16),
            whole,
            pltpu.VMEM((2 * size, parcels), bf16),
            pltpu.VMEM((GROUPS * 2 * size, parcels), bf16),
            whole,
            whole,
            pltpu.VMEM(tiles.shape, bf16),
            pltpu.VMEM((parcels // WIDE * species, WIDE), bf16),
            whole,
            pltpu.SemaphoreType.DMA((9,)),
            pltpu.SemaphoreType.DMA((batches, 2)),
            pltpu.SemaphoreType.DMA((parcels // WIDE,)),
        ],
        compiler_params=params(LIMIT),
        cost_estimate=CHEAP,
    )(neighbours, slots, yields, loss, gathered, weights, comp, chosen, mixed, start, rates, tiles)


def after(values, gates):
    both = lax.optimization_barrier(tuple(values) + tuple(gates))
    return both[: len(values)], both[len(values) :]


def hop(sides):
    size = lax.axis_size("grp")
    right = [(i, (i + 1) % size) for i in range(size)]
    left = [(i, (i - 1) % size) for i in range(size)]
    return lax.ppermute(sides[0], "grp", right), lax.ppermute(sides[1], "grp", left)


def rows(sides, first, size):
    return tuple(side[first : first + size] for side in sides)


def halves_of(sides):
    half = sides[0].shape[0] // 32 * 16
    return sides[0][:half], sides[1][half:]


SIZES = (112, 48)


def shards(
    composition,
    neighbours,
    mixing_weights,
    slot_order,
    photo_index,
    photo_table,
    coupling,
    loss_rate,
    preconditioner,
):
    parcels, species = composition.shape
    blocks = parcels // BLOCK
    ring_size = lax.axis_size("grp")
    comp = composition.T
    firsts = [sum(SIZES[:i]) for i in range(len(SIZES))]
    place = neighbours // blocks
    distance = (lax.axis_index("grp") - place) % ring_size
    codes = distance * blocks + neighbours % blocks

    pieces = [comp[first : first + size] for first, size in zip(firsts, SIZES)]
    a_own = pieces[0].astype(bf16)
    (b_piece,), (a_own,) = after(pieces[1:], (a_own,))
    b_own = b_piece.astype(bf16)
    gathered = lax.all_gather(a_own, "grp", axis=0)
    b_one = hop((b_own, b_own))
    (tiles_in, photo_in), b_one = after(
        (preconditioner, photo_index.reshape(blocks, BLOCK)), b_one
    )
    packed = pack(tiles_in, photo_in)
    arrived = lax.all_to_all(packed, "band", split_axis=0, concat_axis=0, tiled=True)
    b_two = hop(b_one)
    chosen = select(slot_order)
    b_two, (chosen,) = after(b_two, (chosen,))
    b_three = hop(b_two)
    (arrived,), b_three = after((arrived,), b_three)
    tiles, rates = unpack(arrived, photo_table.T)
    b_four = hop(halves_of(b_three))
    parts = [b_own, b_one[0], b_two[0], b_three[0], b_three[1], b_two[1], b_one[1], *b_four]
    mixed_b = mix(
        firsts[1], SIZES[1], codes, mixing_weights, comp, slot_order, chosen, parts
    )
    (gathered,), gates = after((gathered,), (tiles, rates, *mixed_b))
    tiles, rates, *mixed_b = gates
    updated = finish(
        neighbours, slot_order, coupling.T, loss_rate.reshape(species, 1),
        gathered, mixing_weights, comp, chosen, *mixed_b, rates, tiles,
    )
    return updated.T


def solution(mesh):
    placed = (
        P(("band", "grp"), None),
        P(("band", "grp"), None),
        P(("band", "grp"), None, None, None),
        P(("band", "grp"), None),
        P(("band", "grp")),
        P(),
        P(),
        P(),
        P(("band", "grp"), None, None),
    )
    return jax.shard_map(
        shards, mesh=mesh, in_specs=placed, out_specs=P(("band", "grp"), None), check_vma=False
    )
```

```python
import functools

import jax
import jax.numpy as jnp
from jax import lax
from jax.experimental import pallas as pl
from jax.experimental.pallas import tpu as pltpu
from jax.sharding import PartitionSpec as P

BLOCK = 128
NEWTON = 2
WIDE = 256
LIMIT = 60
GROUPS = 2
LOT = 8
time_step = 0.5

f32 = jnp.float32
bf16 = jnp.bfloat16
VMEM = pl.BlockSpec(memory_space=pltpu.VMEM)
SMEM = pl.BlockSpec(memory_space=pltpu.SMEM)
ANY = pl.BlockSpec(memory_space=pl.ANY)


CHEAP = pl.CostEstimate(flops=1, bytes_accessed=1, transcendentals=0)


def params(mib):
    return pltpu.CompilerParams(vmem_limit_bytes=mib << 20)


def halves(values):
    high = values.astype(bf16)
    return high, (values - high.astype(f32)).astype(bf16)


def pack_kernel(tiles_ref, photo_ref, out_ref):
    count, species, _ = tiles_ref.shape
    rest = species - BLOCK
    fold = BLOCK // rest
    rows = species // fold

    def body(t, _):
        tile = tiles_ref[t]
        out_ref[t, pl.ds(0, species), :] = tile[:, :BLOCK]
        out_ref[t, pl.ds(species, rows), :] = jnp.concatenate(
            [tile[i * rows : (i + 1) * rows, BLOCK:] for i in range(fold)], axis=1
        )
        entries = photo_ref[pl.ds(t, 1), :].astype(f32)
        out_ref[t, pl.ds(species + rows, 8), :] = jnp.broadcast_to(entries, (8, BLOCK))
        return 0

    lax.fori_loop(0, count, body, 0, unroll=2)


def pack(tiles, photo):
    count, species, _ = tiles.shape
    rows = species + species * (species - BLOCK) // BLOCK + 8
    return pl.pallas_call(
        pack_kernel,
        out_shape=jax.ShapeDtypeStruct((count, rows, BLOCK), f32),
        grid=(count // LOT,),
        in_specs=[
            pl.BlockSpec((LOT, species, species), lambda i: (i, 0, 0)),
            pl.BlockSpec((LOT, BLOCK), lambda i: (i, 0)),
        ],
        out_specs=pl.BlockSpec((LOT, rows, BLOCK), lambda i: (i, 0, 0)),
        compiler_params=params(LIMIT),
        cost_estimate=CHEAP,
    )(tiles, photo)


def unpack_kernel(packed_ref, table_ref, tiles_ref, rates_ref):
    count = packed_ref.shape[0]
    species = rates_ref.shape[0]
    levels = table_ref.shape[1]
    rest = species - BLOCK
    fold = BLOCK // rest
    rows = species // fold
    t_high, t_rest = halves(table_ref[...])
    first = table_ref[...] - t_high.astype(f32)
    t_low = (first - t_rest.astype(f32)).astype(bf16)
    table = jnp.concatenate([t_high, t_rest, t_low], axis=1)

    def body(t, _):
        folded = packed_ref[t, pl.ds(species, rows), :]
        tail = jnp.concatenate(
            [folded[:, i * rest : (i + 1) * rest] for i in range(fold)], axis=0
        )
        tile = jnp.concatenate([packed_ref[t, pl.ds(0, species), :], tail], axis=1)
        high, low = halves(tile.T)
        tiles_ref[t] = jnp.concatenate([high, low, high], axis=1)
        entries = packed_ref[t, pl.ds(species + rows, 1), :].astype(jnp.int32)
        level = lax.broadcasted_iota(jnp.int32, (levels, BLOCK), 0)
        onehot = (level == entries).astype(f32).astype(bf16)
        onehot = jnp.concatenate([onehot, onehot, onehot], axis=0)
        rates_ref[:, pl.ds(pl.multiple_of(t * BLOCK, BLOCK), BLOCK)] = jnp.dot(
            table, onehot, preferred_element_type=f32
        )
        return 0

    lax.fori_loop(0, count, body, 0, unroll=2)


def unpack(packed, table):
    count = packed.shape[0]
    species = table.shape[0]
    return pl.pallas_call(
        unpack_kernel,
        out_shape=(
            jax.ShapeDtypeStruct((count, species, 3 * species), bf16),
            jax.ShapeDtypeStruct((species, count * BLOCK), f32),
        ),
        grid=(count // LOT,),
        in_specs=[
            pl.BlockSpec((LOT,) + packed.shape[1:], lambda i: (i, 0, 0)),
            pl.BlockSpec(table.shape, lambda i: (0, 0)),
        ],
        out_specs=(
            pl.BlockSpec((LOT, species, 3 * species), lambda i: (i, 0, 0)),
            pl.BlockSpec((species, LOT * BLOCK), lambda i: (0, i)),
        ),
        compiler_params=params(LIMIT),
        cost_estimate=CHEAP,
    )(packed, table)


def select_kernel(slots_ref, out_ref):
    parcels = slots_ref.shape[1]

    def body(t, _):
        off = pl.multiple_of(t * WIDE, WIDE)
        place = slots_ref[:, pl.ds(off, WIDE)] & (WIDE - 1)
        lane = lax.broadcasted_iota(jnp.int32, (WIDE, WIDE), 0)
        out_ref[pl.ds(off, WIDE), :] = (lane == place).astype(f32).T.astype(bf16)
        return 0

    lax.fori_loop(0, parcels // WIDE, body, 0)


def select(slots):
    parcels = slots.shape[1]
    return pl.pallas_call(
        select_kernel,
        out_shape=jax.ShapeDtypeStruct((parcels, WIDE), bf16),
        in_specs=[VMEM],
        out_specs=VMEM,
        compiler_params=params(LIMIT),
        cost_estimate=CHEAP,
    )(slots)


def mix_kernel(first, size, count, *refs):
    codes_ref, slots_ref, weights_ref, comp_ref, select_ref = refs[:5]
    parts = refs[5 : 5 + count]
    mixed_ref, start_ref, held, own, weights, chosen, both, stack, sems = refs[5 + count :]
    parcels = mixed_ref.shape[1]
    blocks = parcels // BLOCK
    wide = parcels // WIDE
    half = size // 32 * 16
    lots = 4
    lot = blocks // lots
    copies = []
    for place in range(7):
        spot = place if place < 4 else place + 1
        copies.append((parts[place], held.at[spot]))
    copies.append((parts[7], held.at[4, pl.ds(0, half), :]))
    copies.append((parts[8], held.at[4, pl.ds(half, size - half), :]))
    copies.append((comp_ref.at[pl.ds(first, size), :], own))
    early = len(copies)
    for n in range(lots):
        copies.append((weights_ref.at[pl.ds(n * lot, lot)], weights.at[pl.ds(n * lot, lot)]))
    copies.append((select_ref, chosen))
    copies = [
        pltpu.make_async_copy(source, target, sems.at[i])
        for i, (source, target) in enumerate(copies)
    ]
    for copy in copies:
        copy.start()
    for copy in copies[:early]:
        copy.wait()

    def mix(c, _):
        picked = []
        for k in range(weights.shape[1]):
            code = codes_ref[c, k]
            column = pl.multiple_of((code & (blocks - 1)) * BLOCK, BLOCK)
            picked.append(held[lax.div(code, blocks), :, pl.ds(column, BLOCK)])
        rows = jnp.concatenate(picked, axis=1)
        block = jnp.concatenate([weights[c, k] for k in range(weights.shape[1])], axis=1)
        term = lax.dot_general(
            rows, block, (((1,), (1,)), ((), ())), preferred_element_type=f32
        )
        off = pl.multiple_of(c * BLOCK, BLOCK)
        mixed_ref[:, pl.ds(off, BLOCK)] = own[:, pl.ds(off, BLOCK)] + term
        return 0

    for n in range(lots):
        copies[early + n].wait()
        lax.fori_loop(n * lot, (n + 1) * lot, mix, 0, unroll=lot)
    high, low = halves(mixed_ref[...])
    both[pl.ds(0, size), :] = high
    both[pl.ds(size, size), :] = low
    copies[early + lots].wait()

    def move(i, _):
        group = slots_ref[...] >> 8
        for j in range(GROUPS):
            keep = (group == i * GROUPS + j).astype(f32).astype(bf16)
            stack[pl.ds(j * 2 * size, 2 * size), :] = both[...] * keep
        moved = jnp.dot(stack[...], chosen[...], preferred_element_type=f32)
        for j in range(GROUPS):
            at = j * 2 * size
            off = pl.multiple_of((i * GROUPS + j) * WIDE, WIDE)
            start_ref[:, pl.ds(off, WIDE)] = (
                moved[at : at + size] + moved[at + size : at + 2 * size]
            )
        return 0

    lax.fori_loop(0, wide // GROUPS, move, 0)


def mix(first, size, codes, weights, comp, slots, chosen, parts):
    parcels = comp.shape[1]
    shape = jax.ShapeDtypeStruct((size, parcels), f32)
    return pl.pallas_call(
        functools.partial(mix_kernel, first, size, len(parts)),
        out_shape=(shape, shape),
        in_specs=[SMEM, VMEM] + [ANY] * (3 + len(parts)),
        out_specs=(VMEM, VMEM),
        scratch_shapes=[
            pltpu.VMEM((8, size, parcels), bf16),
            pltpu.VMEM((size, parcels), f32),
            pltpu.VMEM(weights.shape, bf16),
            pltpu.VMEM(chosen.shape, bf16),
            pltpu.VMEM((2 * size, parcels), bf16),
            pltpu.VMEM((GROUPS * 2 * size, parcels), bf16),
            pltpu.SemaphoreType.DMA((15,)),
        ],
        compiler_params=params(LIMIT),
        cost_estimate=CHEAP,
    )(codes, slots, weights, comp, chosen, *parts)


BATCH = 16


def finish_kernel(
    near_ref, slots_ref, yields_ref, loss_ref,
    gathered_ref, weights_ref, comp_ref, select_ref, mixed_ref, start_ref, rates_ref, tiles_ref,
    out_ref,
    held, weights, chosen, home, both, stack, begun, rates_in, tiles, delta, result,
    sems, lot_sems, out_sems,
):
    species, parcels = rates_in.shape
    size = held.shape[1]
    blocks = parcels // BLOCK
    wide = parcels // WIDE
    span = BATCH * BLOCK
    batches = parcels // span
    lots = 4
    lot = blocks // lots
    rest = species - size
    first_copies = [
        pltpu.make_async_copy(gathered_ref, held, sems.at[0]),
        pltpu.make_async_copy(
            comp_ref.at[pl.ds(0, size), :], home.at[pl.ds(0, size), :], sems.at[1]
        ),
    ]
    weight_copies = [
        pltpu.make_async_copy(
            weights_ref.at[pl.ds(n * lot, lot)], weights.at[pl.ds(n * lot, lot)], sems.at[2 + n]
        )
        for n in range(lots)
    ]
    select_copy = pltpu.make_async_copy(select_ref, chosen, sems.at[2 + lots])
    home_copy = pltpu.make_async_copy(
        mixed_ref, home.at[pl.ds(size, rest), :], sems.at[3 + lots]
    )
    start_copy = pltpu.make_async_copy(
        start_ref, begun.at[pl.ds(size, rest), :], sems.at[4 + lots]
    )
    lot_copies = []
    for b in range(batches):
        column = pl.ds(b * span, span)
        lot_copies.append(
            pltpu.make_async_copy(
                rates_ref.at[:, column], rates_in.at[:, column], lot_sems.at[b, 0]
            )
        )
        lot_copies.append(
            pltpu.make_async_copy(
                tiles_ref.at[pl.ds(b * BATCH, BATCH)],
                tiles.at[pl.ds(b * BATCH, BATCH)],
                lot_sems.at[b, 1],
            )
        )
    for copy in (
        first_copies + weight_copies + [select_copy, start_copy] + lot_copies + [home_copy]
    ):
        copy.start()
    for copy in first_copies:
        copy.wait()

    def mix(c, _):
        picked = []
        for k in range(weights.shape[1]):
            block = near_ref[c, k]
            column = pl.multiple_of((block & (blocks - 1)) * BLOCK, BLOCK)
            picked.append(held[lax.div(block, blocks), :, pl.ds(column, BLOCK)])
        rows = jnp.concatenate(picked, axis=1)
        block = jnp.concatenate([weights[c, k] for k in range(weights.shape[1])], axis=1)
        term = lax.dot_general(
            rows, block, (((1,), (1,)), ((), ())), preferred_element_type=f32
        )
        off = pl.multiple_of(c * BLOCK, BLOCK)
        total = home[pl.ds(0, size), pl.ds(off, BLOCK)] + term
        home[pl.ds(0, size), pl.ds(off, BLOCK)] = total
        high, low = halves(total)
        both[pl.ds(0, size), pl.ds(off, BLOCK)] = high
        both[pl.ds(size, size), pl.ds(off, BLOCK)] = low
        return 0

    for n in range(lots):
        weight_copies[n].wait()
        lax.fori_loop(n * lot, (n + 1) * lot, mix, 0, unroll=lot)
    select_copy.wait()

    group = slots_ref[...] >> 8

    def lay(i):
        for j in range(GROUPS):
            keep = (group == i * GROUPS + j).astype(f32).astype(bf16)
            stack[i % 2, pl.ds(j * 2 * size, 2 * size), :] = both[...] * keep

    lay(0)
    for i in range(wide // GROUPS):
        if i + 1 < wide // GROUPS:
            lay(i + 1)
        moved = jnp.dot(stack[i % 2], chosen[...], preferred_element_type=f32)
        for j in range(GROUPS):
            at = j * 2 * size
            off = (i * GROUPS + j) * WIDE
            begun[pl.ds(0, size), pl.ds(off, WIDE)] = (
                moved[at : at + size] + moved[at + size : at + 2 * size]
            )

    start_copy.wait()
    home_copy.wait()
    for copy in lot_copies:
        copy.wait()
    y_high, y_low = halves(yields_ref[...])
    yields = jnp.concatenate([y_high, y_low, y_high], axis=1)
    loss = loss_ref[...]

    def spread(values):
        high, low = halves(values)
        return jnp.concatenate([high, high, low], axis=0)

    for b in range(batches):
        off = b * span
        start = begun[:, pl.ds(off, span)]
        rates = rates_in[:, pl.ds(off, span)]
        current = start
        for newton_step in range(NEWTON):
            forcing = (
                jnp.dot(yields, spread(current * rates), preferred_element_type=f32)
                - loss * current * current
            )
            defect = current - start - time_step * forcing
            wings = spread(defect)
            update = [
                jnp.dot(
                    tiles[b * BATCH + i],
                    wings[:, i * BLOCK : (i + 1) * BLOCK],
                    preferred_element_type=f32,
                )
                for i in range(BATCH)
            ]
            current = current - jnp.concatenate(update, axis=1)
        change = (current - start).astype(bf16)
        for i in range(span // WIDE):
            delta[pl.ds((b * span // WIDE + i) * species, species), :] = change[
                :, i * WIDE : (i + 1) * WIDE
            ]

    outs = []
    for t in range(wide):
        off = t * WIDE
        slots = slots_ref[:, pl.ds(off, WIDE)]
        lane = lax.broadcasted_iota(jnp.int32, (WIDE, WIDE), 0)
        picks = (lane == (slots & (WIDE - 1))).astype(f32).astype(bf16)
        group = slots >> 8
        total = jnp.zeros((species, WIDE), f32)
        for j in range(wide):
            moved = jnp.dot(
                delta[pl.ds(j * species, species), :], picks, preferred_element_type=f32
            )
            total = jnp.where(group == j, moved, total)
        result[:, pl.ds(off, WIDE)] = home[:, pl.ds(off, WIDE)] + total
        out = pltpu.make_async_copy(
            result.at[:, pl.ds(off, WIDE)], out_ref.at[:, pl.ds(off, WIDE)], out_sems.at[t]
        )
        out.start()
        outs.append(out)
    for out in outs:
        out.wait()


def finish(neighbours, slots, yields, loss, gathered, weights, comp, chosen, mixed, start, rates, tiles):
    species, parcels = rates.shape
    size = gathered.shape[1]
    batches = parcels // (BATCH * BLOCK)
    whole = pltpu.VMEM((species, parcels), f32)
    return pl.pallas_call(
        finish_kernel,
        out_shape=jax.ShapeDtypeStruct((species, parcels), f32),
        in_specs=[SMEM] + [VMEM] * 3 + [ANY] * 8,
        out_specs=ANY,
        scratch_shapes=[
            pltpu.VMEM(gathered.shape, bf16),
            pltpu.VMEM(weights.shape, bf16),
            pltpu.VMEM(chosen.shape, bf16),
            whole,
            pltpu.VMEM((2 * size, parcels), bf16),
            pltpu.VMEM((2, GROUPS * 2 * size, parcels), bf16),
            whole,
            whole,
            pltpu.VMEM(tiles.shape, bf16),
            pltpu.VMEM((parcels // WIDE * species, WIDE), bf16),
            whole,
            pltpu.SemaphoreType.DMA((9,)),
            pltpu.SemaphoreType.DMA((batches, 2)),
            pltpu.SemaphoreType.DMA((parcels // WIDE,)),
        ],
        compiler_params=params(LIMIT),
        cost_estimate=CHEAP,
    )(neighbours, slots, yields, loss, gathered, weights, comp, chosen, mixed, start, rates, tiles)


def after(values, gates):
    both = lax.optimization_barrier(tuple(values) + tuple(gates))
    return both[: len(values)], both[len(values) :]


def hop(sides):
    size = lax.axis_size("grp")
    right = [(i, (i + 1) % size) for i in range(size)]
    left = [(i, (i - 1) % size) for i in range(size)]
    return lax.ppermute(sides[0], "grp", right), lax.ppermute(sides[1], "grp", left)


def rows(sides, first, size):
    return tuple(side[first : first + size] for side in sides)


def halves_of(sides):
    half = sides[0].shape[0] // 32 * 16
    return sides[0][:half], sides[1][half:]


SIZES = (112, 48)


def shards(
    composition,
    neighbours,
    mixing_weights,
    slot_order,
    photo_index,
    photo_table,
    coupling,
    loss_rate,
    preconditioner,
):
    parcels, species = composition.shape
    blocks = parcels // BLOCK
    ring_size = lax.axis_size("grp")
    comp = composition.T
    firsts = [sum(SIZES[:i]) for i in range(len(SIZES))]
    place = neighbours // blocks
    distance = (lax.axis_index("grp") - place) % ring_size
    codes = distance * blocks + neighbours % blocks

    pieces = [comp[first : first + size] for first, size in zip(firsts, SIZES)]
    a_own = pieces[0].astype(bf16)
    (b_piece,), (a_own,) = after(pieces[1:], (a_own,))
    b_own = b_piece.astype(bf16)
    gathered = lax.all_gather(a_own, "grp", axis=0)
    b_one = hop((b_own, b_own))
    (tiles_in, photo_in), b_one = after(
        (preconditioner, photo_index.reshape(blocks, BLOCK)), b_one
    )
    packed = pack(tiles_in, photo_in)
    arrived = lax.all_to_all(packed, "band", split_axis=0, concat_axis=0, tiled=True)
    b_two = hop(b_one)
    chosen = select(slot_order)
    b_two, (chosen,) = after(b_two, (chosen,))
    b_three = hop(b_two)
    (arrived,), b_three = after((arrived,), b_three)
    tiles, rates = unpack(arrived, photo_table.T)
    b_four = hop(halves_of(b_three))
    parts = [b_own, b_one[0], b_two[0], b_three[0], b_three[1], b_two[1], b_one[1], *b_four]
    mixed_b = mix(
        firsts[1], SIZES[1], codes, mixing_weights, comp, slot_order, chosen, parts
    )
    (gathered,), gates = after((gathered,), (tiles, rates, *mixed_b))
    tiles, rates, *mixed_b = gates
    updated = finish(
        neighbours, slot_order, coupling.T, loss_rate.reshape(species, 1),
        gathered, mixing_weights, comp, chosen, *mixed_b, rates, tiles,
    )
    return updated.T


def solution(mesh):
    placed = (
        P(("band", "grp"), None),
        P(("band", "grp"), None),
        P(("band", "grp"), None, None, None),
        P(("band", "grp"), None),
        P(("band", "grp")),
        P(),
        P(),
        P(),
        P(("band", "grp"), None, None),
    )
    return jax.shard_map(
        shards, mesh=mesh, in_specs=placed, out_specs=P(("band", "grp"), None), check_vma=False
    )
```

```python
import functools

import jax
import jax.numpy as jnp
from jax import lax
from jax.experimental import pallas as pl
from jax.experimental.pallas import tpu as pltpu
from jax.sharding import PartitionSpec as P

BLOCK = 128
NEWTON = 2
WIDE = 256
LIMIT = 60
GROUPS = 2
LOT = 8
time_step = 0.5

f32 = jnp.float32
bf16 = jnp.bfloat16
f8 = jnp.float8_e4m3fn
LOW_SCALE = 128.0
VMEM = pl.BlockSpec(memory_space=pltpu.VMEM)
SMEM = pl.BlockSpec(memory_space=pltpu.SMEM)
ANY = pl.BlockSpec(memory_space=pl.ANY)


CHEAP = pl.CostEstimate(flops=1, bytes_accessed=1, transcendentals=0)


def params(mib):
    return pltpu.CompilerParams(vmem_limit_bytes=mib << 20)


def halves(values):
    high = values.astype(bf16)
    return high, (values - high.astype(f32)).astype(bf16)


def pack_kernel(tiles_ref, photo_ref, out_ref):
    count, species, _ = tiles_ref.shape
    rest = species - BLOCK
    fold = BLOCK // rest
    rows = species // fold

    def body(t, _):
        tile = tiles_ref[t]
        out_ref[t, pl.ds(0, species), :] = tile[:, :BLOCK]
        out_ref[t, pl.ds(species, rows), :] = jnp.concatenate(
            [tile[i * rows : (i + 1) * rows, BLOCK:] for i in range(fold)], axis=1
        )
        entries = photo_ref[pl.ds(t, 1), :].astype(f32)
        out_ref[t, pl.ds(species + rows, 8), :] = jnp.broadcast_to(entries, (8, BLOCK))
        return 0

    lax.fori_loop(0, count, body, 0, unroll=2)


def pack(tiles, photo):
    count, species, _ = tiles.shape
    rows = species + species * (species - BLOCK) // BLOCK + 8
    return pl.pallas_call(
        pack_kernel,
        out_shape=jax.ShapeDtypeStruct((count, rows, BLOCK), f32),
        grid=(count // LOT,),
        in_specs=[
            pl.BlockSpec((LOT, species, species), lambda i: (i, 0, 0)),
            pl.BlockSpec((LOT, BLOCK), lambda i: (i, 0)),
        ],
        out_specs=pl.BlockSpec((LOT, rows, BLOCK), lambda i: (i, 0, 0)),
        compiler_params=params(LIMIT),
        cost_estimate=CHEAP,
    )(tiles, photo)


def unpack_kernel(packed_ref, table_ref, tiles_ref, rates_ref):
    count = packed_ref.shape[0]
    species = rates_ref.shape[0]
    levels = table_ref.shape[1]
    rest = species - BLOCK
    fold = BLOCK // rest
    rows = species // fold
    t_high, t_rest = halves(table_ref[...])
    first = table_ref[...] - t_high.astype(f32)
    t_low = (first - t_rest.astype(f32)).astype(bf16)
    table = jnp.concatenate([t_high, t_rest, t_low], axis=1)

    def body(t, _):
        folded = packed_ref[t, pl.ds(species, rows), :]
        tail = jnp.concatenate(
            [folded[:, i * rest : (i + 1) * rest] for i in range(fold)], axis=0
        )
        tile = jnp.concatenate([packed_ref[t, pl.ds(0, species), :], tail], axis=1)
        high, low = halves(tile.T)
        tiles_ref[t] = jnp.concatenate([high, low, high], axis=1)
        entries = packed_ref[t, pl.ds(species + rows, 1), :].astype(jnp.int32)
        level = lax.broadcasted_iota(jnp.int32, (levels, BLOCK), 0)
        onehot = (level == entries).astype(f32).astype(bf16)
        onehot = jnp.concatenate([onehot, onehot, onehot], axis=0)
        rates_ref[:, pl.ds(pl.multiple_of(t * BLOCK, BLOCK), BLOCK)] = jnp.dot(
            table, onehot, preferred_element_type=f32
        )
        return 0

    lax.fori_loop(0, count, body, 0, unroll=2)


def unpack(packed, table):
    count = packed.shape[0]
    species = table.shape[0]
    return pl.pallas_call(
        unpack_kernel,
        out_shape=(
            jax.ShapeDtypeStruct((count, species, 3 * species), bf16),
            jax.ShapeDtypeStruct((species, count * BLOCK), f32),
        ),
        grid=(count // LOT,),
        in_specs=[
            pl.BlockSpec((LOT,) + packed.shape[1:], lambda i: (i, 0, 0)),
            pl.BlockSpec(table.shape, lambda i: (0, 0)),
        ],
        out_specs=(
            pl.BlockSpec((LOT, species, 3 * species), lambda i: (i, 0, 0)),
            pl.BlockSpec((species, LOT * BLOCK), lambda i: (0, i)),
        ),
        compiler_params=params(LIMIT),
        cost_estimate=CHEAP,
    )(packed, table)


def select_kernel(slots_ref, out_ref):
    parcels = slots_ref.shape[1]

    def body(t, _):
        off = pl.multiple_of(t * WIDE, WIDE)
        place = slots_ref[:, pl.ds(off, WIDE)] & (WIDE - 1)
        lane = lax.broadcasted_iota(jnp.int32, (WIDE, WIDE), 0)
        out_ref[pl.ds(off, WIDE), :] = (lane == place).astype(f32).T.astype(bf16)
        return 0

    lax.fori_loop(0, parcels // WIDE, body, 0)


def select(slots):
    parcels = slots.shape[1]
    return pl.pallas_call(
        select_kernel,
        out_shape=jax.ShapeDtypeStruct((parcels, WIDE), bf16),
        in_specs=[VMEM],
        out_specs=VMEM,
        compiler_params=params(LIMIT),
        cost_estimate=CHEAP,
    )(slots)


def mix_kernel(first, size, count, *refs):
    codes_ref, slots_ref, weights_ref, comp_ref, select_ref = refs[:5]
    parts = refs[5 : 5 + count]
    mixed_ref, start_ref, held, own, weights, chosen, both, stack, sems = refs[5 + count :]
    parcels = mixed_ref.shape[1]
    blocks = parcels // BLOCK
    wide = parcels // WIDE
    half = size // 32 * 16
    lots = 4
    lot = blocks // lots
    copies = []
    for place in range(7):
        spot = place if place < 4 else place + 1
        copies.append((parts[place], held.at[spot]))
    copies.append((parts[7], held.at[4, pl.ds(0, half), :]))
    copies.append((parts[8], held.at[4, pl.ds(half, size - half), :]))
    copies.append((comp_ref.at[pl.ds(first, size), :], own))
    early = len(copies)
    for n in range(lots):
        copies.append((weights_ref.at[pl.ds(n * lot, lot)], weights.at[pl.ds(n * lot, lot)]))
    copies.append((select_ref, chosen))
    copies = [
        pltpu.make_async_copy(source, target, sems.at[i])
        for i, (source, target) in enumerate(copies)
    ]
    for copy in copies:
        copy.start()
    for copy in copies[:early]:
        copy.wait()

    def mix(c, _):
        picked = []
        for k in range(weights.shape[1]):
            code = codes_ref[c, k]
            column = pl.multiple_of((code & (blocks - 1)) * BLOCK, BLOCK)
            picked.append(held[lax.div(code, blocks), :, pl.ds(column, BLOCK)])
        rows = jnp.concatenate(picked, axis=1)
        block = jnp.concatenate([weights[c, k] for k in range(weights.shape[1])], axis=1)
        term = lax.dot_general(
            rows, block, (((1,), (1,)), ((), ())), preferred_element_type=f32
        )
        off = pl.multiple_of(c * BLOCK, BLOCK)
        mixed_ref[:, pl.ds(off, BLOCK)] = own[:, pl.ds(off, BLOCK)] + term
        return 0

    for n in range(lots):
        copies[early + n].wait()
        lax.fori_loop(n * lot, (n + 1) * lot, mix, 0, unroll=lot)
    high, low = halves(mixed_ref[...])
    both[pl.ds(0, size), :] = high
    both[pl.ds(size, size), :] = low
    copies[early + lots].wait()

    def move(i, _):
        group = slots_ref[...] >> 8
        for j in range(GROUPS):
            keep = (group == i * GROUPS + j).astype(f32).astype(bf16)
            stack[pl.ds(j * 2 * size, 2 * size), :] = both[...] * keep
        moved = jnp.dot(stack[...], chosen[...], preferred_element_type=f32)
        for j in range(GROUPS):
            at = j * 2 * size
            off = pl.multiple_of((i * GROUPS + j) * WIDE, WIDE)
            start_ref[:, pl.ds(off, WIDE)] = (
                moved[at : at + size] + moved[at + size : at + 2 * size]
            )
        return 0

    lax.fori_loop(0, wide // GROUPS, move, 0)


def mix(first, size, codes, weights, comp, slots, chosen, parts):
    parcels = comp.shape[1]
    shape = jax.ShapeDtypeStruct((size, parcels), f32)
    return pl.pallas_call(
        functools.partial(mix_kernel, first, size, len(parts)),
        out_shape=(shape, shape),
        in_specs=[SMEM, VMEM] + [ANY] * (3 + len(parts)),
        out_specs=(VMEM, VMEM),
        scratch_shapes=[
            pltpu.VMEM((8, size, parcels), bf16),
            pltpu.VMEM((size, parcels), f32),
            pltpu.VMEM(weights.shape, bf16),
            pltpu.VMEM(chosen.shape, bf16),
            pltpu.VMEM((2 * size, parcels), bf16),
            pltpu.VMEM((GROUPS * 2 * size, parcels), bf16),
            pltpu.SemaphoreType.DMA((15,)),
        ],
        compiler_params=params(LIMIT),
        cost_estimate=CHEAP,
    )(codes, slots, weights, comp, chosen, *parts)


BATCH = 16


def finish_kernel(
    near_ref, slots_ref, yields_ref, loss_ref,
    gathered_ref, weights_ref, comp_ref, select_ref, mixed_ref, start_ref, rates_ref, tiles_ref,
    out_ref,
    held, weights, chosen, fine, home, both, stack, stack_low, begun, rates_in, tiles, delta, result,
    sems, lot_sems, out_sems,
):
    species, parcels = rates_in.shape
    size = held.shape[1]
    blocks = parcels // BLOCK
    wide = parcels // WIDE
    span = BATCH * BLOCK
    batches = parcels // span
    lots = 4
    lot = blocks // lots
    rest = species - size
    first_copies = [
        pltpu.make_async_copy(gathered_ref, held, sems.at[0]),
        pltpu.make_async_copy(
            comp_ref.at[pl.ds(0, size), :], home.at[pl.ds(0, size), :], sems.at[1]
        ),
    ]
    weight_copies = [
        pltpu.make_async_copy(
            weights_ref.at[pl.ds(n * lot, lot)], weights.at[pl.ds(n * lot, lot)], sems.at[2 + n]
        )
        for n in range(lots)
    ]
    select_copy = pltpu.make_async_copy(select_ref, chosen, sems.at[2 + lots])
    home_copy = pltpu.make_async_copy(
        mixed_ref, home.at[pl.ds(size, rest), :], sems.at[3 + lots]
    )
    start_copy = pltpu.make_async_copy(
        start_ref, begun.at[pl.ds(size, rest), :], sems.at[4 + lots]
    )
    lot_copies = []
    for b in range(batches):
        column = pl.ds(b * span, span)
        lot_copies.append(
            pltpu.make_async_copy(
                rates_ref.at[:, column], rates_in.at[:, column], lot_sems.at[b, 0]
            )
        )
        lot_copies.append(
            pltpu.make_async_copy(
                tiles_ref.at[pl.ds(b * BATCH, BATCH)],
                tiles.at[pl.ds(b * BATCH, BATCH)],
                lot_sems.at[b, 1],
            )
        )
    for copy in (
        first_copies + weight_copies + [select_copy, start_copy] + lot_copies + [home_copy]
    ):
        copy.start()
    for copy in first_copies:
        copy.wait()

    def mix(c, _):
        picked = []
        for k in range(weights.shape[1]):
            block = near_ref[c, k]
            column = pl.multiple_of((block & (blocks - 1)) * BLOCK, BLOCK)
            picked.append(held[lax.div(block, blocks), :, pl.ds(column, BLOCK)])
        rows = jnp.concatenate(picked, axis=1)
        block = jnp.concatenate([weights[c, k] for k in range(weights.shape[1])], axis=1)
        term = lax.dot_general(
            rows, block, (((1,), (1,)), ((), ())), preferred_element_type=f32
        )
        off = pl.multiple_of(c * BLOCK, BLOCK)
        total = home[pl.ds(0, size), pl.ds(off, BLOCK)] + term
        home[pl.ds(0, size), pl.ds(off, BLOCK)] = total
        high, low = halves(total)
        both[pl.ds(0, size), pl.ds(off, BLOCK)] = high
        both[pl.ds(size, size), pl.ds(off, BLOCK)] = low * LOW_SCALE
        return 0

    for n in range(lots):
        weight_copies[n].wait()
        lax.fori_loop(n * lot, (n + 1) * lot, mix, 0, unroll=lot)
    select_copy.wait()

    group = slots_ref[...] >> 8

    fine[...] = chosen[...].astype(f8)

    def lay(i):
        lows = []
        for j in range(GROUPS):
            keep = (group == i * GROUPS + j).astype(f32).astype(bf16)
            stack[i % 2, pl.ds(j * size, size), :] = both[pl.ds(0, size), :] * keep
            lows.append(both[pl.ds(size, size), :] * keep)
        stack_low[i % 2] = jnp.concatenate(lows, axis=0).astype(f8)

    lay(0)
    for i in range(wide // GROUPS):
        if i + 1 < wide // GROUPS:
            lay(i + 1)
        moved = jnp.dot(stack[i % 2], chosen[...], preferred_element_type=f32)
        moved_low = jnp.dot(stack_low[i % 2], fine[...], preferred_element_type=f32)
        for j in range(GROUPS):
            off = (i * GROUPS + j) * WIDE
            begun[pl.ds(0, size), pl.ds(off, WIDE)] = (
                moved[j * size : (j + 1) * size]
                + moved_low[j * size : (j + 1) * size] * (1 / LOW_SCALE)
            )

    start_copy.wait()
    home_copy.wait()
    for copy in lot_copies:
        copy.wait()
    y_high, y_low = halves(yields_ref[...])
    yields = jnp.concatenate([y_high, y_low, y_high], axis=1)
    loss = loss_ref[...]

    def spread(values):
        high, low = halves(values)
        return jnp.concatenate([high, high, low], axis=0)

    for b in range(batches):
        off = b * span
        start = begun[:, pl.ds(off, span)]
        rates = rates_in[:, pl.ds(off, span)]
        current = start
        for newton_step in range(NEWTON):
            forcing = (
                jnp.dot(yields, spread(current * rates), preferred_element_type=f32)
                - loss * current * current
            )
            defect = current - start - time_step * forcing
            wings = spread(defect)
            update = [
                jnp.dot(
                    tiles[b * BATCH + i],
                    wings[:, i * BLOCK : (i + 1) * BLOCK],
                    preferred_element_type=f32,
                )
                for i in range(BATCH)
            ]
            current = current - jnp.concatenate(update, axis=1)
        change = (current - start).astype(bf16)
        for i in range(span // WIDE):
            delta[pl.ds((b * span // WIDE + i) * species, species), :] = change[
                :, i * WIDE : (i + 1) * WIDE
            ]

    outs = []
    for t in range(wide):
        off = t * WIDE
        slots = slots_ref[:, pl.ds(off, WIDE)]
        lane = lax.broadcasted_iota(jnp.int32, (WIDE, WIDE), 0)
        picks = (lane == (slots & (WIDE - 1))).astype(f32).astype(bf16)
        group = slots >> 8
        total = jnp.zeros((species, WIDE), f32)
        for j in range(wide):
            moved = jnp.dot(
                delta[pl.ds(j * species, species), :], picks, preferred_element_type=f32
            )
            total = jnp.where(group == j, moved, total)
        result[:, pl.ds(off, WIDE)] = home[:, pl.ds(off, WIDE)] + total
        out = pltpu.make_async_copy(
            result.at[:, pl.ds(off, WIDE)], out_ref.at[:, pl.ds(off, WIDE)], out_sems.at[t]
        )
        out.start()
        outs.append(out)
    for out in outs:
        out.wait()


def finish(neighbours, slots, yields, loss, gathered, weights, comp, chosen, mixed, start, rates, tiles):
    species, parcels = rates.shape
    size = gathered.shape[1]
    batches = parcels // (BATCH * BLOCK)
    whole = pltpu.VMEM((species, parcels), f32)
    return pl.pallas_call(
        finish_kernel,
        out_shape=jax.ShapeDtypeStruct((species, parcels), f32),
        in_specs=[SMEM] + [VMEM] * 3 + [ANY] * 8,
        out_specs=ANY,
        scratch_shapes=[
            pltpu.VMEM(gathered.shape, bf16),
            pltpu.VMEM(weights.shape, bf16),
            pltpu.VMEM(chosen.shape, bf16),
            pltpu.VMEM(chosen.shape, f8),
            whole,
            pltpu.VMEM((2 * size, parcels), bf16),
            pltpu.VMEM((2, GROUPS * size, parcels), bf16),
            pltpu.VMEM((2, GROUPS * size, parcels), f8),
            whole,
            whole,
            pltpu.VMEM(tiles.shape, bf16),
            pltpu.VMEM((parcels // WIDE * species, WIDE), bf16),
            whole,
            pltpu.SemaphoreType.DMA((9,)),
            pltpu.SemaphoreType.DMA((batches, 2)),
            pltpu.SemaphoreType.DMA((parcels // WIDE,)),
        ],
        compiler_params=params(LIMIT),
        cost_estimate=CHEAP,
    )(neighbours, slots, yields, loss, gathered, weights, comp, chosen, mixed, start, rates, tiles)


def after(values, gates):
    both = lax.optimization_barrier(tuple(values) + tuple(gates))
    return both[: len(values)], both[len(values) :]


def hop(sides):
    size = lax.axis_size("grp")
    right = [(i, (i + 1) % size) for i in range(size)]
    left = [(i, (i - 1) % size) for i in range(size)]
    return lax.ppermute(sides[0], "grp", right), lax.ppermute(sides[1], "grp", left)


def rows(sides, first, size):
    return tuple(side[first : first + size] for side in sides)


def halves_of(sides):
    half = sides[0].shape[0] // 32 * 16
    return sides[0][:half], sides[1][half:]


SIZES = (112, 48)


def shards(
    composition,
    neighbours,
    mixing_weights,
    slot_order,
    photo_index,
    photo_table,
    coupling,
    loss_rate,
    preconditioner,
):
    parcels, species = composition.shape
    blocks = parcels // BLOCK
    ring_size = lax.axis_size("grp")
    comp = composition.T
    firsts = [sum(SIZES[:i]) for i in range(len(SIZES))]
    place = neighbours // blocks
    distance = (lax.axis_index("grp") - place) % ring_size
    codes = distance * blocks + neighbours % blocks

    pieces = [comp[first : first + size] for first, size in zip(firsts, SIZES)]
    a_own = pieces[0].astype(bf16)
    (b_piece,), (a_own,) = after(pieces[1:], (a_own,))
    b_own = b_piece.astype(bf16)
    gathered = lax.all_gather(a_own, "grp", axis=0)
    b_one = hop((b_own, b_own))
    (tiles_in, photo_in), b_one = after(
        (preconditioner, photo_index.reshape(blocks, BLOCK)), b_one
    )
    packed = pack(tiles_in, photo_in)
    arrived = lax.all_to_all(packed, "band", split_axis=0, concat_axis=0, tiled=True)
    b_two = hop(b_one)
    chosen = select(slot_order)
    b_two, (chosen,) = after(b_two, (chosen,))
    b_three = hop(b_two)
    (arrived,), b_three = after((arrived,), b_three)
    tiles, rates = unpack(arrived, photo_table.T)
    b_four = hop(halves_of(b_three))
    parts = [b_own, b_one[0], b_two[0], b_three[0], b_three[1], b_two[1], b_one[1], *b_four]
    mixed_b = mix(
        firsts[1], SIZES[1], codes, mixing_weights, comp, slot_order, chosen, parts
    )
    (gathered,), gates = after((gathered,), (tiles, rates, *mixed_b))
    tiles, rates, *mixed_b = gates
    updated = finish(
        neighbours, slot_order, coupling.T, loss_rate.reshape(species, 1),
        gathered, mixing_weights, comp, chosen, *mixed_b, rates, tiles,
    )
    return updated.T


def solution(mesh):
    placed = (
        P(("band", "grp"), None),
        P(("band", "grp"), None),
        P(("band", "grp"), None, None, None),
        P(("band", "grp"), None),
        P(("band", "grp")),
        P(),
        P(),
        P(),
        P(("band", "grp"), None, None),
    )
    return jax.shard_map(
        shards, mesh=mesh, in_specs=placed, out_specs=P(("band", "grp"), None), check_vma=False
    )
```

```python
import functools

import jax
import jax.numpy as jnp
from jax import lax
from jax.experimental import pallas as pl
from jax.experimental.pallas import tpu as pltpu
from jax.sharding import PartitionSpec as P

BLOCK = 128
NEWTON = 2
WIDE = 256
LIMIT = 60
GROUPS = 4
LOT = 8
time_step = 0.5

f32 = jnp.float32
bf16 = jnp.bfloat16
f8 = jnp.float8_e4m3fn
LOW_SCALE = 128.0
VMEM = pl.BlockSpec(memory_space=pltpu.VMEM)
SMEM = pl.BlockSpec(memory_space=pltpu.SMEM)
ANY = pl.BlockSpec(memory_space=pl.ANY)


CHEAP = pl.CostEstimate(flops=1, bytes_accessed=1, transcendentals=0)


def params(mib):
    return pltpu.CompilerParams(vmem_limit_bytes=mib << 20)


def halves(values):
    high = values.astype(bf16)
    return high, (values - high.astype(f32)).astype(bf16)


def pack_kernel(tiles_ref, photo_ref, out_ref):
    count, species, _ = tiles_ref.shape
    rest = species - BLOCK
    fold = BLOCK // rest
    rows = species // fold

    def body(t, _):
        tile = tiles_ref[t]
        out_ref[t, pl.ds(0, species), :] = tile[:, :BLOCK]
        out_ref[t, pl.ds(species, rows), :] = jnp.concatenate(
            [tile[i * rows : (i + 1) * rows, BLOCK:] for i in range(fold)], axis=1
        )
        entries = photo_ref[pl.ds(t, 1), :].astype(f32)
        out_ref[t, pl.ds(species + rows, 8), :] = jnp.broadcast_to(entries, (8, BLOCK))
        return 0

    lax.fori_loop(0, count, body, 0, unroll=2)


def pack(tiles, photo):
    count, species, _ = tiles.shape
    rows = species + species * (species - BLOCK) // BLOCK + 8
    return pl.pallas_call(
        pack_kernel,
        out_shape=jax.ShapeDtypeStruct((count, rows, BLOCK), f32),
        grid=(count // LOT,),
        in_specs=[
            pl.BlockSpec((LOT, species, species), lambda i: (i, 0, 0)),
            pl.BlockSpec((LOT, BLOCK), lambda i: (i, 0)),
        ],
        out_specs=pl.BlockSpec((LOT, rows, BLOCK), lambda i: (i, 0, 0)),
        compiler_params=params(LIMIT),
        cost_estimate=CHEAP,
    )(tiles, photo)


def unpack_kernel(packed_ref, table_ref, tiles_ref, rates_ref):
    count = packed_ref.shape[0]
    species = rates_ref.shape[0]
    levels = table_ref.shape[1]
    rest = species - BLOCK
    fold = BLOCK // rest
    rows = species // fold
    t_high, t_rest = halves(table_ref[...])
    first = table_ref[...] - t_high.astype(f32)
    t_low = (first - t_rest.astype(f32)).astype(bf16)
    table = jnp.concatenate([t_high, t_rest, t_low], axis=1)

    def body(t, _):
        folded = packed_ref[t, pl.ds(species, rows), :]
        tail = jnp.concatenate(
            [folded[:, i * rest : (i + 1) * rest] for i in range(fold)], axis=0
        )
        tile = jnp.concatenate([packed_ref[t, pl.ds(0, species), :], tail], axis=1)
        high, low = halves(tile.T)
        tiles_ref[t] = jnp.concatenate([high, low, high], axis=1)
        entries = packed_ref[t, pl.ds(species + rows, 1), :].astype(jnp.int32)
        level = lax.broadcasted_iota(jnp.int32, (levels, BLOCK), 0)
        onehot = (level == entries).astype(f32).astype(bf16)
        onehot = jnp.concatenate([onehot, onehot, onehot], axis=0)
        rates_ref[:, pl.ds(pl.multiple_of(t * BLOCK, BLOCK), BLOCK)] = jnp.dot(
            table, onehot, preferred_element_type=f32
        )
        return 0

    lax.fori_loop(0, count, body, 0, unroll=2)


def unpack(packed, table):
    count = packed.shape[0]
    species = table.shape[0]
    return pl.pallas_call(
        unpack_kernel,
        out_shape=(
            jax.ShapeDtypeStruct((count, species, 3 * species), bf16),
            jax.ShapeDtypeStruct((species, count * BLOCK), f32),
        ),
        grid=(count // LOT,),
        in_specs=[
            pl.BlockSpec((LOT,) + packed.shape[1:], lambda i: (i, 0, 0)),
            pl.BlockSpec(table.shape, lambda i: (0, 0)),
        ],
        out_specs=(
            pl.BlockSpec((LOT, species, 3 * species), lambda i: (i, 0, 0)),
            pl.BlockSpec((species, LOT * BLOCK), lambda i: (0, i)),
        ),
        compiler_params=params(LIMIT),
        cost_estimate=CHEAP,
    )(packed, table)


def select_kernel(slots_ref, out_ref):
    parcels = slots_ref.shape[1]

    def body(t, _):
        off = pl.multiple_of(t * WIDE, WIDE)
        place = slots_ref[:, pl.ds(off, WIDE)] & (WIDE - 1)
        lane = lax.broadcasted_iota(jnp.int32, (WIDE, WIDE), 0)
        out_ref[pl.ds(off, WIDE), :] = (lane == place).astype(f32).T.astype(bf16)
        return 0

    lax.fori_loop(0, parcels // WIDE, body, 0)


def select(slots):
    parcels = slots.shape[1]
    return pl.pallas_call(
        select_kernel,
        out_shape=jax.ShapeDtypeStruct((parcels, WIDE), bf16),
        in_specs=[VMEM],
        out_specs=VMEM,
        compiler_params=params(LIMIT),
        cost_estimate=CHEAP,
    )(slots)


def mix_kernel(first, size, count, *refs):
    codes_ref, slots_ref, weights_ref, comp_ref, select_ref = refs[:5]
    parts = refs[5 : 5 + count]
    mixed_ref, start_ref, held, own, weights, chosen, both, stack, sems = refs[5 + count :]
    parcels = mixed_ref.shape[1]
    blocks = parcels // BLOCK
    wide = parcels // WIDE
    half = size // 32 * 16
    lots = 4
    lot = blocks // lots
    copies = []
    for place in range(7):
        spot = place if place < 4 else place + 1
        copies.append((parts[place], held.at[spot]))
    copies.append((parts[7], held.at[4, pl.ds(0, half), :]))
    copies.append((parts[8], held.at[4, pl.ds(half, size - half), :]))
    copies.append((comp_ref.at[pl.ds(first, size), :], own))
    early = len(copies)
    for n in range(lots):
        copies.append((weights_ref.at[pl.ds(n * lot, lot)], weights.at[pl.ds(n * lot, lot)]))
    copies.append((select_ref, chosen))
    copies = [
        pltpu.make_async_copy(source, target, sems.at[i])
        for i, (source, target) in enumerate(copies)
    ]
    for copy in copies:
        copy.start()
    for copy in copies[:early]:
        copy.wait()

    def mix(c, _):
        picked = []
        for k in range(weights.shape[1]):
            code = codes_ref[c, k]
            column = pl.multiple_of((code & (blocks - 1)) * BLOCK, BLOCK)
            picked.append(held[lax.div(code, blocks), :, pl.ds(column, BLOCK)])
        rows = jnp.concatenate(picked, axis=1)
        block = jnp.concatenate([weights[c, k] for k in range(weights.shape[1])], axis=1)
        term = lax.dot_general(
            rows, block, (((1,), (1,)), ((), ())), preferred_element_type=f32
        )
        off = pl.multiple_of(c * BLOCK, BLOCK)
        mixed_ref[:, pl.ds(off, BLOCK)] = own[:, pl.ds(off, BLOCK)] + term
        return 0

    for n in range(lots):
        copies[early + n].wait()
        lax.fori_loop(n * lot, (n + 1) * lot, mix, 0, unroll=lot)
    high, low = halves(mixed_ref[...])
    both[pl.ds(0, size), :] = high
    both[pl.ds(size, size), :] = low
    copies[early + lots].wait()

    def move(i, _):
        group = slots_ref[...] >> 8
        for j in range(GROUPS):
            keep = (group == i * GROUPS + j).astype(f32).astype(bf16)
            stack[pl.ds(j * 2 * size, 2 * size), :] = both[...] * keep
        moved = jnp.dot(stack[...], chosen[...], preferred_element_type=f32)
        for j in range(GROUPS):
            at = j * 2 * size
            off = pl.multiple_of((i * GROUPS + j) * WIDE, WIDE)
            start_ref[:, pl.ds(off, WIDE)] = (
                moved[at : at + size] + moved[at + size : at + 2 * size]
            )
        return 0

    lax.fori_loop(0, wide // GROUPS, move, 0)


def mix(first, size, codes, weights, comp, slots, chosen, parts):
    parcels = comp.shape[1]
    shape = jax.ShapeDtypeStruct((size, parcels), f32)
    return pl.pallas_call(
        functools.partial(mix_kernel, first, size, len(parts)),
        out_shape=(shape, shape),
        in_specs=[SMEM, VMEM] + [ANY] * (3 + len(parts)),
        out_specs=(VMEM, VMEM),
        scratch_shapes=[
            pltpu.VMEM((8, size, parcels), bf16),
            pltpu.VMEM((size, parcels), f32),
            pltpu.VMEM(weights.shape, bf16),
            pltpu.VMEM(chosen.shape, bf16),
            pltpu.VMEM((2 * size, parcels), bf16),
            pltpu.VMEM((GROUPS * 2 * size, parcels), bf16),
            pltpu.SemaphoreType.DMA((15,)),
        ],
        compiler_params=params(LIMIT),
        cost_estimate=CHEAP,
    )(codes, slots, weights, comp, chosen, *parts)


BATCH = 16


def finish_kernel(
    near_ref, slots_ref, yields_ref, loss_ref,
    gathered_ref, weights_ref, comp_ref, select_ref, mixed_ref, start_ref, rates_ref, tiles_ref,
    out_ref,
    held, weights, chosen, fine, home, both, stack, stack_low, begun, rates_in, tiles, delta, result,
    sems, lot_sems, out_sems,
):
    species, parcels = rates_in.shape
    size = held.shape[1]
    blocks = parcels // BLOCK
    wide = parcels // WIDE
    span = BATCH * BLOCK
    batches = parcels // span
    lots = 4
    lot = blocks // lots
    rest = species - size
    first_copies = [
        pltpu.make_async_copy(gathered_ref, held, sems.at[0]),
        pltpu.make_async_copy(
            comp_ref.at[pl.ds(0, size), :], home.at[pl.ds(0, size), :], sems.at[1]
        ),
    ]
    weight_copies = [
        pltpu.make_async_copy(
            weights_ref.at[pl.ds(n * lot, lot)], weights.at[pl.ds(n * lot, lot)], sems.at[2 + n]
        )
        for n in range(lots)
    ]
    select_copy = pltpu.make_async_copy(select_ref, chosen, sems.at[2 + lots])
    home_copy = pltpu.make_async_copy(
        mixed_ref, home.at[pl.ds(size, rest), :], sems.at[3 + lots]
    )
    start_copy = pltpu.make_async_copy(
        start_ref, begun.at[pl.ds(size, rest), :], sems.at[4 + lots]
    )
    lot_copies = []
    for b in range(batches):
        column = pl.ds(b * span, span)
        lot_copies.append(
            pltpu.make_async_copy(
                rates_ref.at[:, column], rates_in.at[:, column], lot_sems.at[b, 0]
            )
        )
        lot_copies.append(
            pltpu.make_async_copy(
                tiles_ref.at[pl.ds(b * BATCH, BATCH)],
                tiles.at[pl.ds(b * BATCH, BATCH)],
                lot_sems.at[b, 1],
            )
        )
    for copy in (
        first_copies + weight_copies + [select_copy, start_copy] + lot_copies + [home_copy]
    ):
        copy.start()
    for copy in first_copies:
        copy.wait()

    def mix(c, _):
        picked = []
        for k in range(weights.shape[1]):
            block = near_ref[c, k]
            column = pl.multiple_of((block & (blocks - 1)) * BLOCK, BLOCK)
            picked.append(held[lax.div(block, blocks), :, pl.ds(column, BLOCK)])
        rows = jnp.concatenate(picked, axis=1)
        block = jnp.concatenate([weights[c, k] for k in range(weights.shape[1])], axis=1)
        term = lax.dot_general(
            rows, block, (((1,), (1,)), ((), ())), preferred_element_type=f32
        )
        off = pl.multiple_of(c * BLOCK, BLOCK)
        total = home[pl.ds(0, size), pl.ds(off, BLOCK)] + term
        home[pl.ds(0, size), pl.ds(off, BLOCK)] = total
        high, low = halves(total)
        both[pl.ds(0, size), pl.ds(off, BLOCK)] = high
        both[pl.ds(size, size), pl.ds(off, BLOCK)] = low * LOW_SCALE
        return 0

    for n in range(lots):
        weight_copies[n].wait()
        lax.fori_loop(n * lot, (n + 1) * lot, mix, 0, unroll=lot)
    select_copy.wait()

    group = slots_ref[...] >> 8

    fine[...] = chosen[...].astype(f8)

    def lay(i):
        lows = []
        for j in range(GROUPS):
            keep = (group == i * GROUPS + j).astype(f32).astype(bf16)
            stack[i % 2, pl.ds(j * size, size), :] = both[pl.ds(0, size), :] * keep
            lows.append(both[pl.ds(size, size), :] * keep)
        stack_low[i % 2] = jnp.concatenate(lows, axis=0).astype(f8)

    lay(0)
    for i in range(wide // GROUPS):
        if i + 1 < wide // GROUPS:
            lay(i + 1)
        moved = jnp.dot(stack[i % 2], chosen[...], preferred_element_type=f32)
        moved_low = jnp.dot(stack_low[i % 2], fine[...], preferred_element_type=f32)
        for j in range(GROUPS):
            off = (i * GROUPS + j) * WIDE
            begun[pl.ds(0, size), pl.ds(off, WIDE)] = (
                moved[j * size : (j + 1) * size]
                + moved_low[j * size : (j + 1) * size] * (1 / LOW_SCALE)
            )

    start_copy.wait()
    home_copy.wait()
    for copy in lot_copies:
        copy.wait()
    y_high, y_low = halves(yields_ref[...])
    yields = jnp.concatenate([y_high, y_low, y_high], axis=1)
    loss = loss_ref[...]

    def spread(values):
        high, low = halves(values)
        return jnp.concatenate([high, high, low], axis=0)

    for b in range(batches):
        off = b * span
        start = begun[:, pl.ds(off, span)]
        rates = rates_in[:, pl.ds(off, span)]
        current = start
        for newton_step in range(NEWTON):
            forcing = (
                jnp.dot(yields, spread(current * rates), preferred_element_type=f32)
                - loss * current * current
            )
            defect = -time_step * forcing
            if newton_step > 0:
                defect = current - start + defect
            wings = spread(defect)
            update = [
                jnp.dot(
                    tiles[b * BATCH + i],
                    wings[:, i * BLOCK : (i + 1) * BLOCK],
                    preferred_element_type=f32,
                )
                for i in range(BATCH)
            ]
            current = current - jnp.concatenate(update, axis=1)
        change = (current - start).astype(bf16)
        for i in range(span // WIDE):
            delta[pl.ds((b * span // WIDE + i) * species, species), :] = change[
                :, i * WIDE : (i + 1) * WIDE
            ]

    outs = []
    for t in range(wide):
        off = t * WIDE
        slots = slots_ref[:, pl.ds(off, WIDE)]
        lane = lax.broadcasted_iota(jnp.int32, (WIDE, WIDE), 0)
        picks = (lane == (slots & (WIDE - 1))).astype(f32).astype(bf16)
        group = slots >> 8
        total = jnp.zeros((species, WIDE), f32)
        for j in range(wide):
            moved = jnp.dot(
                delta[pl.ds(j * species, species), :], picks, preferred_element_type=f32
            )
            total = jnp.where(group == j, moved, total)
        result[:, pl.ds(off, WIDE)] = home[:, pl.ds(off, WIDE)] + total
        out = pltpu.make_async_copy(
            result.at[:, pl.ds(off, WIDE)], out_ref.at[:, pl.ds(off, WIDE)], out_sems.at[t]
        )
        out.start()
        outs.append(out)
    for out in outs:
        out.wait()


def finish(neighbours, slots, yields, loss, gathered, weights, comp, chosen, mixed, start, rates, tiles):
    species, parcels = rates.shape
    size = gathered.shape[1]
    batches = parcels // (BATCH * BLOCK)
    whole = pltpu.VMEM((species, parcels), f32)
    return pl.pallas_call(
        finish_kernel,
        out_shape=jax.ShapeDtypeStruct((species, parcels), f32),
        in_specs=[SMEM] + [VMEM] * 3 + [ANY] * 8,
        out_specs=ANY,
        scratch_shapes=[
            pltpu.VMEM(gathered.shape, bf16),
            pltpu.VMEM(weights.shape, bf16),
            pltpu.VMEM(chosen.shape, bf16),
            pltpu.VMEM(chosen.shape, f8),
            whole,
            pltpu.VMEM((2 * size, parcels), bf16),
            pltpu.VMEM((2, GROUPS * size, parcels), bf16),
            pltpu.VMEM((2, GROUPS * size, parcels), f8),
            whole,
            whole,
            pltpu.VMEM(tiles.shape, bf16),
            pltpu.VMEM((parcels // WIDE * species, WIDE), bf16),
            whole,
            pltpu.SemaphoreType.DMA((9,)),
            pltpu.SemaphoreType.DMA((batches, 2)),
            pltpu.SemaphoreType.DMA((parcels // WIDE,)),
        ],
        compiler_params=params(LIMIT),
        cost_estimate=CHEAP,
    )(neighbours, slots, yields, loss, gathered, weights, comp, chosen, mixed, start, rates, tiles)


def after(values, gates):
    both = lax.optimization_barrier(tuple(values) + tuple(gates))
    return both[: len(values)], both[len(values) :]


def hop(sides):
    size = lax.axis_size("grp")
    right = [(i, (i + 1) % size) for i in range(size)]
    left = [(i, (i - 1) % size) for i in range(size)]
    return lax.ppermute(sides[0], "grp", right), lax.ppermute(sides[1], "grp", left)


def rows(sides, first, size):
    return tuple(side[first : first + size] for side in sides)


def halves_of(sides):
    half = sides[0].shape[0] // 32 * 16
    return sides[0][:half], sides[1][half:]


SIZES = (112, 48)


def shards(
    composition,
    neighbours,
    mixing_weights,
    slot_order,
    photo_index,
    photo_table,
    coupling,
    loss_rate,
    preconditioner,
):
    parcels, species = composition.shape
    blocks = parcels // BLOCK
    ring_size = lax.axis_size("grp")
    comp = composition.T
    firsts = [sum(SIZES[:i]) for i in range(len(SIZES))]
    place = neighbours // blocks
    distance = (lax.axis_index("grp") - place) % ring_size
    codes = distance * blocks + neighbours % blocks

    pieces = [comp[first : first + size] for first, size in zip(firsts, SIZES)]
    a_own = pieces[0].astype(bf16)
    (b_piece,), (a_own,) = after(pieces[1:], (a_own,))
    b_own = b_piece.astype(bf16)
    gathered = lax.all_gather(a_own, "grp", axis=0)
    b_one = hop((b_own, b_own))
    (tiles_in, photo_in), b_one = after(
        (preconditioner, photo_index.reshape(blocks, BLOCK)), b_one
    )
    packed = pack(tiles_in, photo_in)
    arrived = lax.all_to_all(packed, "band", split_axis=0, concat_axis=0, tiled=True)
    b_two = hop(b_one)
    chosen = select(slot_order)
    b_two, (chosen,) = after(b_two, (chosen,))
    b_three = hop(b_two)
    (arrived,), b_three = after((arrived,), b_three)
    tiles, rates = unpack(arrived, photo_table.T)
    b_four = hop(halves_of(b_three))
    parts = [b_own, b_one[0], b_two[0], b_three[0], b_three[1], b_two[1], b_one[1], *b_four]
    mixed_b = mix(
        firsts[1], SIZES[1], codes, mixing_weights, comp, slot_order, chosen, parts
    )
    (gathered,), gates = after((gathered,), (tiles, rates, *mixed_b))
    tiles, rates, *mixed_b = gates
    updated = finish(
        neighbours, slot_order, coupling.T, loss_rate.reshape(species, 1),
        gathered, mixing_weights, comp, chosen, *mixed_b, rates, tiles,
    )
    return updated.T


def solution(mesh):
    placed = (
        P(("band", "grp"), None),
        P(("band", "grp"), None),
        P(("band", "grp"), None, None, None),
        P(("band", "grp"), None),
        P(("band", "grp")),
        P(),
        P(),
        P(),
        P(("band", "grp"), None, None),
    )
    return jax.shard_map(
        shards, mesh=mesh, in_specs=placed, out_specs=P(("band", "grp"), None), check_vma=False
    )
```
